32 devices in a mesh: section: 2 (over x), fsdp: 4 (over y, core), expert: 4 (over z).
Axes of the slice: x: 2, y: 2, z: 4, core: 2. Of those that a mesh axis runs over, the one named last changes fastest.
Arguments:
- x_in: bfloat16 [2, 4096, 1536], P(None, ('fsdp', 'expert')), may hold values from -6 to 6
- cotangent: bfloat16 [2, 4096, 1536], P(None, ('fsdp', 'expert')), may hold values from -6 to 6
- seg_ids: int32 [2, 4096], P(None, 'fsdp'), may hold values from 0 to 8, as said below
- routes: int32 [2, 2, 4096, 8], P('section', None, ('fsdp', 'expert')), may hold values from 0 to 19, all different within a row; in each aligned block of 256 rows (0 to 255, 256 to 511, ..., all dimensions but the last counted through in order) at most 146 rows name the same one
- query_key_value_weight: bfloat16 [2, 1536, 2560], P('section', ('fsdp', 'expert')), may hold values from -0.15625 to 0.15625
- w_out: bfloat16 [2, 1536, 1536], P('section', ('fsdp', 'expert')), may hold values from -1.25 to 1.25
- w_router: bfloat16 [2, 1536, 20], P('section', ('fsdp', 'expert')), may hold values from -0.078125 to 0.078125
- norm1_gain: bfloat16 [2, 1536], P('section', ('fsdp', 'expert')), may hold values from 0.5 to 1.5
- norm2_gain: bfloat16 [2, 1536], P('section', ('fsdp', 'expert')), may hold values from 0.5 to 1.5
- w_gate_up: bfloat16 [2, 20, 1536, 1024], P('section', 'expert', 'fsdp'), may hold values from -0.15625 to 0.15625
- w_down: bfloat16 [2, 20, 512, 1536], P('section', 'expert', 'fsdp'), may hold values from -0.75 to 0.75
Outputs:
- section_out: bfloat16 [2, 2, 4096, 1536], P('section', None, ('fsdp', 'expert'))
- in_grad: bfloat16 [2, 2, 4096, 1536], P('section', None, ('fsdp', 'expert'))
- grad_qkv: float32 [2, 1536, 2560], P('section', ('fsdp', 'expert'))
- grad_out: float32 [2, 1536, 1536], P('section', ('fsdp', 'expert'))
- grad_router: float32 [2, 1536, 20], P('section', ('fsdp', 'expert'))
- grad_gain_one: float32 [2, 1536], P('section', ('fsdp', 'expert'))
- grad_gain_two: float32 [2, 1536], P('section', ('fsdp', 'expert'))
- grad_gate_up: float32 [2, 20, 1536, 1024], P('section', 'expert', 'fsdp')
- grad_down: float32 [2, 20, 512, 1536], P('section', 'expert', 'fsdp')
The draws below stay inside these ranges and needn't reach their ends.
Inputs may be any that keep to these rules, and one draw needn't show every extreme that they name: `seg_ids`: in each group of 1024 tokens the first 512 are 0 (the prompt); the rest run from 1 to 8 without falling, each value present. `routes`: each row names 8 different experts; among the 256 rows of one device for one section and micro-batch, no expert is named more than 146 times.
All inputs are finite; a program needn't handle non-finite values.
Results may differ from the reference program's by a relative error of at most 0.022.
Values may be sent and summed in bfloat16 or wider, within the bound.
A program may use at most 640 MiB of HBM per device.

```python
import math
from functools import partial
import jax
import jax.numpy as jnp
import numpy as np
from jax import lax

MODEL_WIDTH = 1536
QUERY_HEADS = 24
KEY_VALUE_HEADS = 8
HEAD_SIZE = 64
FF = 512
TOPK = 8
NCONT = 8
MB = 2
GROUP_TOKENS = 1024
NE = 20
T_DEV = 256
TOKENS = 4096
CAP = 146


def draw_seg_ids(key, part):
    key = jax.random.fold_in(key, 7)
    prompt_groups = MB * (TOKENS // GROUP_TOKENS)
    half = GROUP_TOKENS // 2
    key_rows = jax.random.split(key, prompt_groups)

    def one_group(group_key):
        picks = jax.random.permutation(group_key, half - 1)[:NCONT - 1] + 1
        cuts = jnp.sort(picks.astype(jnp.int32))
        place = jnp.arange(half, dtype=jnp.int32)
        later = 1 + jnp.sum((cuts[None, :] <= place[:, None]).astype(jnp.int32), 1)
        return jnp.concatenate([jnp.zeros((GROUP_TOKENS - half,), jnp.int32), later])
    return jax.vmap(one_group)(key_rows).reshape(MB, TOKENS)


def shard_levels(stream_key, extent, shards, smallest, largest):
    loudness, own = 1.0, jax.random.fold_in(stream_key, 6)
    for dim, blocks in shards:
        heights = jnp.exp(jax.random.uniform(jax.random.fold_in(own, dim), (blocks,), jnp.float32, smallest / len(shards), largest / len(shards)))
        loudness = loudness * jnp.repeat(heights, extent[dim] // blocks).reshape([-1 if axis == dim else 1 for axis in range(len(extent))])
    return loudness


def deal_out(stream_key, own, number, rows, amount, top, reach, lean):
    order = jax.random.permutation(stream_key, amount)
    packed, ordinary = shares(amount, rows * top, reach, lean, True), shares(amount, rows * top, reach, lean, False)
    places = jnp.arange(amount)

    def named(tallies, turn):
        used = int((tallies > 0).sum())
        fixed = max(1, used // 4)
        shifted = fixed + (places - fixed + turn * (used - fixed)) % max(1, amount - fixed)
        return jnp.zeros((amount,), jnp.int32).at[order[jnp.where(places < fixed, places, shifted)]].set(jnp.asarray(tallies, jnp.int32))

    tallies = jnp.where(number % 4 == 0, named(packed, number // 4), named(ordinary, number - number // 4 - 1))
    mixed = jax.random.permutation(jax.random.fold_in(own, 3), amount)
    source_of, taker = mixed[0:amount // 2 * 2:2], mixed[1:amount // 2 * 2:2]
    room = jnp.minimum(tallies[source_of] - 1, reach - tallies[taker]) // 2
    room = jnp.where((source_of == order[0]) | (taker == order[0]) | (tallies[taker] == 0), 0, jnp.maximum(room, 0))
    shifted = jax.random.randint(jax.random.fold_in(own, 4), (amount // 2,), 0, 1 << 20) % (room + 1)
    tallies = tallies.at[source_of].add(-shifted).at[taker].add(shifted)
    members = jnp.searchsorted(jnp.cumsum(tallies), jnp.arange(rows * top), side="right").astype(jnp.int32)
    table = members.reshape(top, rows).T
    table = table[jax.random.permutation(jax.random.fold_in(own, 1), rows)]
    turn = jax.random.randint(jax.random.fold_in(own, 2), (rows, 1), 0, top)
    return jnp.take_along_axis(table, (jnp.arange(top)[None, :] + turn) % top, axis=1)


def shares(number_of, total, reach, lean, full):
    loads = [(1 << 20) // math.isqrt(grade ** lean) + 1 for grade in range(1, number_of + 1)]
    largest = reach if full else min(reach, max(-(-total // number_of), total * loads[0] // sum(loads)))
    least = 1 if total - largest >= number_of - 1 else 0
    holding, rest = [largest] + [least] * (number_of - 1), total - largest - least * (number_of - 1)
    while rest > 0:
        free = [i for i in range(1, number_of) if holding[i] < largest] or [i for i in range(1, number_of) if holding[i] < reach]
        mass, remaining = sum([loads[i] for i in free]), rest
        for i in free:
            addition = min(reach - holding[i], max(1, remaining * loads[i] // mass), rest)
            holding[i] = holding[i] + addition
            rest = rest - addition
    return np.array(holding)


def bell_draw(key, extent, deviation, reach, shards=(), kind=jnp.bfloat16):
    loudness = shard_levels(key, extent, shards, -0.22, 0.18) if shards else 1.0
    entries = jax.random.normal(key, extent, jnp.float32) * deviation * loudness
    return jnp.minimum(jnp.maximum(entries, -reach), reach).astype(kind)


def setup_inputs(seed: int = 0) -> dict:
    streams_of = jax.random.split(jax.random.key(seed), 12)
    x_in = bell_draw(streams_of[0], (MB, TOKENS, MODEL_WIDTH), 1.0, 6.0, ((1, 16),))
    cotangent = bell_draw(streams_of[1], (MB, TOKENS, MODEL_WIDTH), 1.0, 6.0, ((1, 16),))
    seg_ids = draw_seg_ids(jax.random.fold_in(streams_of[11], 71), 0)
    routes_keys = jax.random.split(jax.random.fold_in(streams_of[3], 1), 2 * MB * TOKENS // T_DEV)
    routes_turns = jax.random.permutation(jax.random.fold_in(streams_of[3], 3), 2 * MB * TOKENS // T_DEV)
    routes = jax.vmap(lambda own, number: deal_out(jax.random.fold_in(streams_of[3], 2), own, number, T_DEV, NE, TOPK, CAP, 1))(routes_keys, routes_turns).reshape((2, MB, TOKENS, TOPK))
    query_key_value_weight = bell_draw(streams_of[4], (2, MODEL_WIDTH, (QUERY_HEADS + 2 * KEY_VALUE_HEADS) * HEAD_SIZE), MODEL_WIDTH ** -0.5, 0.15625, ((0, 2), (1, 16)))
    w_out = bell_draw(streams_of[5], (2, QUERY_HEADS * HEAD_SIZE, MODEL_WIDTH), (MODEL_WIDTH // 64) ** -0.5, 1.25, ((0, 2), (1, 16)))
    w_router = bell_draw(streams_of[6], (2, MODEL_WIDTH, NE), (4 * MODEL_WIDTH) ** -0.5, 0.078125, ((0, 2), (1, 16)))
    norm1_gain = jnp.clip(1.0 + 0.1 * jax.random.normal(streams_of[7], (2, MODEL_WIDTH), jnp.float32), 0.5, 1.5).astype(jnp.bfloat16)
    norm2_gain = jnp.clip(1.0 + 0.1 * jax.random.normal(streams_of[8], (2, MODEL_WIDTH), jnp.float32), 0.5, 1.5).astype(jnp.bfloat16)
    w_gate_up = bell_draw(streams_of[9], (2, NE, MODEL_WIDTH, 2 * FF), MODEL_WIDTH ** -0.5, 0.15625, ((0, 2), (1, 4), (2, 4)))
    w_down = bell_draw(streams_of[10], (2, NE, FF, MODEL_WIDTH), (FF // 8) ** -0.5, 0.75, ((0, 2), (1, 4), (2, 4)))
    return dict(x_in=x_in, cotangent=cotangent, seg_ids=seg_ids, routes=routes, query_key_value_weight=query_key_value_weight, w_out=w_out, w_router=w_router, norm1_gain=norm1_gain, norm2_gain=norm2_gain, w_gate_up=w_gate_up, w_down=w_down)


EPS = 1e-06
THETA = 10000.0
HIGH = lax.Precision.HIGHEST

@jax.custom_vjp
def low(v):
    return lax.optimization_barrier(v.astype(jnp.bfloat16)).astype(jnp.float32)

@jax.custom_vjp
def low_back(v):
    return v

def low_keep(v):
    return (low(v), None)

def low_pass(kept, grad):
    return (grad,)

def back_keep(v):
    return (v, None)

def back_low(kept, grad):
    return (low(grad),)
low.defvjp(low_keep, low_pass)
low_back.defvjp(back_keep, back_low)

def group_positions(segment):
    prompt_group = segment.shape[0]
    labels = jnp.arange(NCONT + 1, dtype=jnp.int32)
    member = (segment[:, None] == labels[None, :]).astype(jnp.int32)
    totals = lax.optimization_barrier(jnp.sum(member, 0))
    starts = jnp.cumsum(totals) - totals
    first = lax.optimization_barrier(jnp.sum(member * starts[None, :], 1))
    place = jnp.arange(prompt_group, dtype=jnp.int32)
    position = jnp.where(segment == 0, place, totals[0] + place - first)
    allowed = (place[None, :] <= place[:, None]) & ((segment[None, :] == 0) | (segment[None, :] == segment[:, None]))
    return (position, allowed)

def apply_rotation(value_rows, position):
    half = value_rows.shape[-1] // 2
    freq = THETA ** (-jnp.arange(half, dtype=jnp.float32) / half)
    angle = position.astype(jnp.float32)[:, None] * freq[None, :]
    cosine_table = jnp.cos(angle)[:, None, :]
    sine_table = jnp.sin(angle)[:, None, :]
    first = value_rows[..., :half]
    second = value_rows[..., half:]
    return jnp.concatenate([first * cosine_table - second * sine_table, second * cosine_table + first * sine_table], -1)

def attend(pieces):
    query_rows, key_rows, value_rows, segment = pieces
    position, allowed = group_positions(segment)
    query_rows = low(apply_rotation(query_rows, position))
    key_rows = low(apply_rotation(key_rows, position))
    prompt_group = query_rows.shape[0]
    group_reshaped = query_rows.reshape(prompt_group, KEY_VALUE_HEADS, QUERY_HEADS // KEY_VALUE_HEADS, HEAD_SIZE)
    raw = jnp.einsum('tkgd,skd->kgts', group_reshaped, key_rows, precision=HIGH) * HEAD_SIZE ** (-0.5)
    raw = low_back(raw)
    masked = jnp.where(allowed[None, None], raw, -1e+30)
    attention_probabilities = low(jax.nn.softmax(masked, axis=-1))
    return jnp.einsum('znbh,hzl->bznl', attention_probabilities, value_rows, precision=HIGH).reshape(prompt_group, QUERY_HEADS * HEAD_SIZE)

def build_tables(route):
    count = route.shape[0]
    flat = route.reshape(-1)
    total = flat.shape[0]
    hot = (flat[:, None] == jnp.arange(NE, dtype=jnp.int32)[None, :]).astype(jnp.int32)
    rank = lax.optimization_barrier(jnp.sum((jnp.cumsum(hot, 0) - hot) * hot, 1))
    depth = CAP * (count // T_DEV)
    order = jnp.arange(total, dtype=jnp.int32)
    table = jnp.full((NE, depth), count, jnp.int32).at[flat, rank].set(order // TOPK)
    gate_index = jnp.full((NE, depth), total, jnp.int32).at[flat, rank].set(order)
    return (table, gate_index)

def rms_norm(value_rows, gain):
    return value_rows * lax.rsqrt(lax.optimization_barrier(jnp.mean(value_rows * value_rows, -1, keepdims=True)) + EPS) * gain

def layer(segment, tables, route, tokens, query_key_value_weight, w_out, w_router, gain_one, gain_two, w_gate_up, w_down):
    table, gate_index = tables
    count, width = tokens.shape
    normed = low(rms_norm(tokens, gain_one))
    attention_mixture = low_back(jnp.dot(normed, query_key_value_weight, precision=HIGH))
    query_columns = QUERY_HEADS * HEAD_SIZE
    key_columns = KEY_VALUE_HEADS * HEAD_SIZE
    prompt_groups = count // GROUP_TOKENS
    query_rows = attention_mixture[:, :query_columns].reshape(prompt_groups, GROUP_TOKENS, QUERY_HEADS, HEAD_SIZE)
    key_rows = attention_mixture[:, query_columns:query_columns + key_columns].reshape(prompt_groups, GROUP_TOKENS, KEY_VALUE_HEADS, HEAD_SIZE)
    value_rows = low(attention_mixture[:, query_columns + key_columns:]).reshape(prompt_groups, GROUP_TOKENS, KEY_VALUE_HEADS, HEAD_SIZE)
    attended = lax.map(jax.checkpoint(attend), (query_rows, key_rows, value_rows, segment.reshape(prompt_groups, GROUP_TOKENS)))
    attended = low(low_back(attended.reshape(count, query_columns)))
    hidden = tokens + low_back(jnp.dot(attended, w_out, precision=HIGH))
    normed_two = low(rms_norm(hidden, gain_two))
    logits = low_back(jnp.dot(normed_two, w_router, precision=HIGH))
    gates = jax.nn.softmax(jnp.take_along_axis(logits, route, 1), axis=-1)
    padded = jnp.concatenate([normed_two, jnp.zeros((1, width), normed_two.dtype)], 0)

    def expert(pieces):
        index, gate_up, down = pieces
        token_rows = low_back(padded[index])
        both = low_back(jnp.dot(token_rows, gate_up, precision=HIGH))
        act = low(jax.nn.silu(both[:, :FF]) * both[:, FF:])
        return low(low_back(jnp.dot(act, down, precision=HIGH)))
    produced = lax.map(jax.checkpoint(expert), (table, w_gate_up, w_down))
    gate_flat = jnp.concatenate([gates.reshape(-1), jnp.zeros((1,), gates.dtype)])
    weighted = gate_flat[gate_index][:, :, None] * produced
    moe = jnp.zeros((count + 1, width), tokens.dtype).at[table.reshape(-1)].add(weighted.reshape(-1, width))
    return hidden + moe[:count]

def reference(x_in, cotangent, seg_ids, routes, query_key_value_weight, w_out, w_router, norm1_gain, norm2_gain, w_gate_up, w_down):
    arrays = (query_key_value_weight, w_out, w_router, norm1_gain, norm2_gain, w_gate_up, w_down)
    weights = [tuple((a[s].astype(jnp.float32) for a in arrays)) for s in range(2)]
    sums = [tuple((jnp.zeros_like(w) for w in weights[s])) for s in range(2)]
    outputs = [[], []]
    grads_in = [[], []]
    for micro in range(MB):
        segment = seg_ids[micro]
        first_fn = partial(layer, segment, build_tables(routes[0, micro]), routes[0, micro])
        second_fn = partial(layer, segment, build_tables(routes[1, micro]), routes[1, micro])
        first_out, first_pull = jax.vjp(first_fn, x_in[micro].astype(jnp.float32), *weights[0])
        first_sent = first_out.astype(jnp.bfloat16)
        second_out, second_pull = jax.vjp(second_fn, first_sent.astype(jnp.float32), *weights[1])
        second_grads = second_pull(cotangent[micro].astype(jnp.float32))
        back_sent = second_grads[0].astype(jnp.bfloat16)
        first_grads = first_pull(back_sent.astype(jnp.float32))
        outputs[0].append(first_sent)
        outputs[1].append(second_out.astype(jnp.bfloat16))
        grads_in[0].append(first_grads[0].astype(jnp.bfloat16))
        grads_in[1].append(back_sent)
        sums[0] = tuple((a + b for a, b in zip(sums[0], first_grads[1:])))
        sums[1] = tuple((a + b for a, b in zip(sums[1], second_grads[1:])))
    section_out = jnp.stack([jnp.stack(outputs[0]), jnp.stack(outputs[1])])
    in_grad = jnp.stack([jnp.stack(grads_in[0]), jnp.stack(grads_in[1])])
    stacked = [jnp.stack([sums[0][i], sums[1][i]]) for i in range(7)]
    return (section_out, in_grad, stacked[0], stacked[1], stacked[2], stacked[3], stacked[4], stacked[5], stacked[6])
```

```python
import functools

import jax
import jax.numpy as jnp
from jax import lax
from jax.experimental import pallas as pl
from jax.experimental.pallas import tpu as pltpu
from jax.sharding import PartitionSpec as P

QUERY_HEADS = 24
KEY_VALUE_HEADS = 8
HEAD_SIZE = 64
FF = 512
NCONT = 8
EPS = 1e-06
THETA = 10000.0
LANES = 128
LOW = 64

F32 = jnp.float32
BF16 = jnp.bfloat16
ACROSS = (((1,), (1,)), ((), ()))


def swap(block, axis, bit):
    return lax.ppermute(block, axis, [(i, i ^ bit) for i in range(lax.axis_size(axis))])


def onward(block, axis):
    n = lax.axis_size(axis)
    return lax.ppermute(block, axis, [(i, (i + 1) % n) for i in range(n)])


def bits_of(axis):
    bits, bit = [], lax.axis_size(axis) // 2
    while bit:
        bits.append(bit)
        bit //= 2
    return bits


def pick(block, index, axis=0):
    return lax.dynamic_index_in_dim(block, index, axis, keepdims=False)


def after(block, *others):
    return lax.optimization_barrier((block, *others))[0]


def tie(block, *others):
    def body(*refs):
        pass

    return pl.pallas_call(
        body,
        out_shape=jax.ShapeDtypeStruct(block.shape, block.dtype),
        in_specs=[pl.BlockSpec(memory_space=pl.ANY)] * (1 + len(others)),
        out_specs=pl.BlockSpec(memory_space=pl.ANY),
        input_output_aliases={0: 0},
        cost_estimate=pl.CostEstimate(flops=0, bytes_accessed=0, transcendentals=0),
    )(block, *others)


def dense_pieces(block, y_first):
    n = lax.axis_size("expert")
    bits = bits_of("fsdp")
    early, late = (bits[:-1], bits[-1:]) if y_first else ([], bits)
    held = [(0, block)]
    for bit in early:
        held += [(mask ^ bit, swap(b, "fsdp", bit)) for mask, b in held]
    pieces = [(mask, 0, b) for mask, b in held]
    moving = held
    for step in range(1, n):
        moving = [(mask, onward(b, "expert")) for mask, b in moving]
        pieces += [(mask, step, b) for mask, b in moving]
    for bit in late:
        pieces += [(mask ^ bit, step, swap(b, "fsdp", bit)) for mask, step, b in pieces]
    rows, columns = block.shape
    if rows % 16 == 0:
        return pieces
    whole = jnp.zeros((lax.axis_size("fsdp") * n * rows, columns), block.dtype)
    fsdp, expert = lax.axis_index("fsdp"), lax.axis_index("expert")
    for mask, step, b in pieces:
        start = ((fsdp ^ mask) * n + lax.rem(expert - step + n, n)) * rows
        whole = lax.dynamic_update_slice_in_dim(whole, b, start, 0)
    return [(0, 0, whole)]


class Pieces:
    def __init__(self, pieces):
        self.spots = [(mask, step) for mask, step, _ in pieces]
        self.blocks = [b for _, _, b in pieces]
        self.rows, self.columns = self.blocks[0].shape
        self.count = len(self.blocks)

    def copies(self, refs, whole, sems):
        n = lax.axis_size("expert")
        fsdp, expert = lax.axis_index("fsdp"), lax.axis_index("expert")
        out = []
        for k, (mask, step) in enumerate(self.spots):
            if self.count == 1:
                out.append(pltpu.make_async_copy(refs[k], whole, sems.at[k]))
                continue
            start = ((fsdp ^ mask) * n + lax.rem(expert - step + n, n)) * self.rows
            rows = pl.ds(pl.multiple_of(start, self.rows), self.rows)
            out.append(pltpu.make_async_copy(refs[k], whole.at[rows, :], sems.at[k]))
        return out


def vmem_call(body, out_shape, operands, anywhere, scratch_shapes=(), any_out=0, flops=0):
    vmem = pl.BlockSpec(memory_space=pltpu.VMEM)
    hbm = pl.BlockSpec(memory_space=pl.ANY)
    size = sum(o.size * o.dtype.itemsize for o in operands)
    return pl.pallas_call(
        body,
        out_shape=out_shape,
        in_specs=[vmem] * (len(operands) - anywhere) + [hbm] * anywhere,
        out_specs=[vmem] * (len(out_shape) - any_out) + [hbm] * any_out,
        scratch_shapes=list(scratch_shapes),
        compiler_params=pltpu.CompilerParams(vmem_limit_bytes=44 * 2**20),
        cost_estimate=pl.CostEstimate(flops=flops, bytes_accessed=size, transcendentals=0),
    )(*operands)


def turned(block, cosine, sine):
    half = HEAD_SIZE // 2
    wide = block.shape[1]
    lane = lax.broadcasted_iota(jnp.int32, block.shape, 1)
    partner = jnp.where(
        lane % HEAD_SIZE < half, pltpu.roll(block, wide - half, 1), pltpu.roll(block, half, 1)
    )
    return block * cosine + partner * sine


def project_body(pieces, n_total, x_ref, cos_ref, sin_ref, *refs):
    weights, refs = refs[: pieces.count], refs[pieces.count :]
    normed_ref, q_ref, kv_ref, small_ref, out_ref, whole, sems, out_sem = refs
    copies = pieces.copies(weights, whole, sems)
    for copy in copies:
        copy.start()
    x = x_ref[...].astype(F32)
    scaled = x * lax.rsqrt(jnp.mean(x * x, -1, keepdims=True) + EPS)
    for copy in copies:
        copy.wait()
    back = pltpu.make_async_copy(whole, out_ref, out_sem)
    back.start()
    columns = pieces.columns - LANES
    small = whole[:, columns:].astype(F32).T
    small_ref[...] = small
    normed = (scaled * small[n_total : n_total + 1, :]).astype(BF16)
    normed_ref[...] = normed
    block = KEY_VALUE_HEADS * HEAD_SIZE
    repeat = block // cos_ref.shape[1]
    cosine = jnp.concatenate([cos_ref[...]] * repeat, 1)
    sine = jnp.concatenate([sin_ref[...]] * repeat, 1)
    count = columns // block
    for k in range(count):
        mixed = jnp.dot(normed, whole[:, k * block : (k + 1) * block], preferred_element_type=F32)
        if k < count - 1:
            mixed = turned(mixed, cosine, sine)
        if k < count - 2:
            q_ref[:, k * block : (k + 1) * block] = mixed.astype(BF16)
        else:
            kv_ref[k - (count - 2)] = mixed.astype(BF16)
    back.wait()


def project(x, tables, pieces, n_total):
    rows, width = x.shape
    block = KEY_VALUE_HEADS * HEAD_SIZE
    columns = pieces.columns
    return vmem_call(
        functools.partial(project_body, pieces, n_total),
        [
            jax.ShapeDtypeStruct((rows, width), BF16),
            jax.ShapeDtypeStruct((rows, QUERY_HEADS * HEAD_SIZE), BF16),
            jax.ShapeDtypeStruct((2, rows, block), BF16),
            jax.ShapeDtypeStruct((LANES, width), F32),
            jax.ShapeDtypeStruct((width, columns), BF16),
        ],
        [x, *tables, *pieces.blocks],
        pieces.count,
        [
            pltpu.VMEM((width, columns), BF16),
            pltpu.SemaphoreType.DMA((pieces.count,)),
            pltpu.SemaphoreType.DMA,
        ],
        1,
        2 * rows * width * columns,
    )


def route_body(pieces, n_total, x_ref, attended_ref, small_ref, route_ref, *refs):
    weights, refs = refs[: pieces.count], refs[pieces.count :]
    hidden_ref, ext_ref, out_ref, whole, sems, out_sem = refs
    copies = pieces.copies(weights, whole, sems)
    for copy in copies:
        copy.start()
    for copy in copies:
        copy.wait()
    back = pltpu.make_async_copy(whole, out_ref, out_sem)
    back.start()
    rows, width = x_ref.shape
    block = 512
    for k in range(0, width, block):
        hidden_ref[:, k : k + block] = x_ref[:, k : k + block].astype(F32) + jnp.dot(
            attended_ref[...], whole[:, k : k + block], preferred_element_type=F32
        )
    hidden = hidden_ref[...]
    scale = lax.rsqrt(jnp.mean(hidden * hidden, -1, keepdims=True) + EPS)
    normed = (hidden * scale * small_ref[n_total + 1 : n_total + 2, :]).astype(BF16)
    ext_ref[:, :width] = normed
    logits = lax.dot_general(
        normed, small_ref[...].astype(BF16), ACROSS, preferred_element_type=F32
    )
    lane = lax.broadcasted_iota(jnp.int32, logits.shape, 1)
    chosen = lane == route_ref[:, 0:1]
    for k in range(1, route_ref.shape[1]):
        chosen = chosen | (lane == route_ref[:, k : k + 1])
    logits = jnp.where(chosen, logits, -1e30)
    weights = jnp.where(chosen, jnp.exp(logits - jnp.max(logits, 1, keepdims=True)), 0.0)
    gates = weights / jnp.sum(weights, 1, keepdims=True)
    high = gates.astype(BF16).astype(F32)
    ext_ref[:, width:] = (high + pltpu.roll(gates - high, LOW, 1)).astype(BF16)
    back.wait()


def route_tokens(x, attended, small, route, pieces, n_total):
    rows, width = x.shape
    return vmem_call(
        functools.partial(route_body, pieces, n_total),
        [
            jax.ShapeDtypeStruct((rows, width), F32),
            jax.ShapeDtypeStruct((rows, width + LANES), BF16),
            jax.ShapeDtypeStruct((width, pieces.columns), BF16),
        ],
        [x, attended, small, route, *pieces.blocks],
        pieces.count,
        [
            pltpu.VMEM((width, pieces.columns), BF16),
            pltpu.SemaphoreType.DMA((pieces.count,)),
            pltpu.SemaphoreType.DMA,
        ],
        1,
        2 * rows * width * pieces.columns,
    )


def joined(lanes):
    lane = lax.broadcasted_iota(jnp.int32, lanes.shape, 1)
    return jnp.where(lane < LOW, lanes + pltpu.roll(lanes, LOW, 1), 0.0)


def route_back_body(
    n_total, own_ref, arriving_ref, hidden_ref, lanes_ref, grad_ref, small_ref, weight_ref,
    grad_hidden_ref, grad_attn_ref, grad_attended_ref, grad_logits_ref, gain_ref,
):
    rows, width = hidden_ref.shape
    gates = joined(lanes_ref[:, width:].astype(F32))
    grad_gates = joined(own_ref[:, width:] + arriving_ref[:, width:].astype(F32))
    grad_logits = gates * (grad_gates - jnp.sum(gates * grad_gates, 1, keepdims=True))
    grad_logits = grad_logits.astype(BF16)
    grad_logits_ref[...] = grad_logits
    grad_normed = (
        own_ref[:, :width]
        + arriving_ref[:, :width].astype(F32)
        + jnp.dot(grad_logits, small_ref[...].astype(BF16), preferred_element_type=F32)
    )
    hidden = hidden_ref[...]
    scale = lax.rsqrt(jnp.mean(hidden * hidden, -1, keepdims=True) + EPS)
    unit = hidden * scale
    gain = jnp.sum(grad_normed * unit, 0, keepdims=True)
    gain_ref[...] = jnp.broadcast_to(gain, gain_ref.shape)
    lifted = grad_normed * small_ref[n_total + 1 : n_total + 2, :]
    grad_hidden = (
        grad_ref[...].astype(F32)
        + scale * lifted
        - unit * (scale * jnp.mean(lifted * unit, -1, keepdims=True))
    )
    grad_hidden_ref[...] = grad_hidden
    grad_attn = grad_hidden.astype(BF16)
    grad_attn_ref[...] = grad_attn
    block = 512
    for k in range(0, width, block):
        grad_attended_ref[:, k : k + block] = lax.dot_general(
            grad_attn, weight_ref[k : k + block, :], ACROSS, preferred_element_type=F32
        ).astype(BF16)


def route_back(own, arriving, hidden, x_ext, grad, small, weight, n_total):
    rows, width = hidden.shape
    return vmem_call(
        functools.partial(route_back_body, n_total),
        [
            jax.ShapeDtypeStruct((rows, width), F32),
            jax.ShapeDtypeStruct((rows, width), BF16),
            jax.ShapeDtypeStruct((rows, weight.shape[0]), BF16),
            jax.ShapeDtypeStruct((rows, LANES), BF16),
            jax.ShapeDtypeStruct((8, width), F32),
        ],
        [own, arriving, hidden, x_ext, grad, small, weight],
        0,
        flops=2 * rows * width * width,
    )


def project_back_body(
    n_total, columns, grad_q_ref, own_ref, arriving_ref, cos_ref, sin_ref, x_ref, grad_hidden_ref, small_ref,
    weight_ref, grad_mixed_ref, grad_x_ref, gain_ref,
):
    rows, width = x_ref.shape
    block = KEY_VALUE_HEADS * HEAD_SIZE
    repeat = block // cos_ref.shape[1]
    cosine = jnp.concatenate([cos_ref[...]] * repeat, 1)
    sine = jnp.concatenate([sin_ref[...]] * repeat, 1)
    grad_keys = own_ref[0].astype(F32) + arriving_ref[0].astype(F32)
    grad_values = own_ref[1].astype(F32) + arriving_ref[1].astype(F32)
    query_columns = columns - 2 * block
    grad_mixed_ref[:, :query_columns] = grad_q_ref[...]
    grad_mixed_ref[:, query_columns : query_columns + block] = turned(grad_keys, cosine, -sine).astype(BF16)
    grad_mixed_ref[:, query_columns + block :] = grad_values.astype(BF16)
    grad_mixed = grad_mixed_ref[...]
    parts = []
    step = 512
    for k in range(0, width, step):
        parts.append(
            lax.dot_general(
                grad_mixed, weight_ref[k : k + step, :columns], ACROSS, preferred_element_type=F32
            )
        )
    grad_normed = jnp.concatenate(parts, 1)
    x = x_ref[...].astype(F32)
    scale = lax.rsqrt(jnp.mean(x * x, -1, keepdims=True) + EPS)
    unit = x * scale
    gain = jnp.sum(grad_normed * unit, 0, keepdims=True)
    gain_ref[...] = jnp.broadcast_to(gain, gain_ref.shape)
    lifted = grad_normed * small_ref[n_total : n_total + 1, :]
    grad_x_ref[...] = (
        grad_hidden_ref[...]
        + scale * lifted
        - unit * (scale * jnp.mean(lifted * unit, -1, keepdims=True))
    ).astype(BF16)


def project_back(grad_q, own, arriving, tables, x, grad_hidden, small, weight, n_total):
    rows, width = x.shape
    columns = weight.shape[1] - LANES
    return vmem_call(
        functools.partial(project_back_body, n_total, columns),
        [
            jax.ShapeDtypeStruct((rows, columns), BF16),
            jax.ShapeDtypeStruct((rows, width), BF16),
            jax.ShapeDtypeStruct((8, width), F32),
        ],
        [grad_q, own, arriving, *tables, x, grad_hidden, small, weight],
        0,
        flops=2 * rows * width * columns,
    )


def product_body(extra, left_ref, right_ref, *refs):
    if extra is None:
        keep_ref, send_ref = refs
    else:
        normed_ref, logits_ref, gain_one_ref, gain_two_ref, keep_ref, send_ref = refs
    role, high = pl.program_id(0), pl.program_id(1)
    rows, columns = keep_ref.shape[1], right_ref.shape[1]
    core = lax.axis_index("fsdp") % 2
    which = high * 2 + jnp.where(role == 0, core, 1 - core)
    spot = pl.ds(pl.multiple_of(which * rows, LANES), rows)

    def fill(out_ref):
        left = left_ref[:, spot].astype(F32).T.astype(BF16)
        step = 512
        for k in range(0, columns, step):
            out_ref[0, :, k : k + step] = jnp.dot(
                left, right_ref[:, k : k + step], preferred_element_type=F32
            ).astype(BF16)
        if extra is not None:
            small = jnp.dot(
                normed_ref[:, spot].astype(F32).T.astype(BF16), logits_ref[...],
                preferred_element_type=F32,
            )
            lane = lax.broadcasted_iota(jnp.int32, small.shape, 1)
            one = gain_one_ref[:, spot].T[:, 0:1]
            two = gain_two_ref[:, spot].T[:, 0:1]
            small = jnp.where(lane == extra, one, jnp.where(lane == extra + 1, two, small))
            out_ref[0, :, columns:] = small.astype(BF16)

    @pl.when(role == 0)
    def _():
        fill(keep_ref)

    @pl.when(role == 1)
    def _():
        fill(send_ref)


def dense_product(left, right, extra=None, others=()):
    tokens, width = left.shape
    highs = lax.axis_size("fsdp") // 2
    rows = width // (2 * highs)
    columns = right.shape[1] + (0 if extra is None else LANES)
    whole = lambda a: pl.BlockSpec(a.shape, lambda r, h: (0,) * a.ndim)
    operands = [left, right, *others]
    half = jax.ShapeDtypeStruct((highs, rows, columns), BF16)
    return pl.pallas_call(
        functools.partial(product_body, extra),
        grid=(2, highs),
        in_specs=[whole(a) for a in operands],
        out_specs=[
            pl.BlockSpec((1, rows, columns), lambda r, h: (jnp.where(r == 0, h, highs - 1), 0, 0)),
            pl.BlockSpec((1, rows, columns), lambda r, h: (jnp.where(r == 0, 0, h), 0, 0)),
        ],
        out_shape=[half, half],
        compiler_params=pltpu.CompilerParams(vmem_limit_bytes=44 * 2**20),
        cost_estimate=pl.CostEstimate(
            flops=2 * tokens * width * columns, bytes_accessed=2 * width * columns, transcendentals=0
        ),
    )(*operands)


def gate_of(lanes, which):
    place_of = lax.broadcasted_iota(jnp.int32, lanes.shape, 1)
    chosen = (place_of == which) | (place_of == which + LOW)
    return jnp.sum(jnp.where(chosen, lanes.astype(F32), 0.0), 1, keepdims=True)


def merged(ref):
    block = ref[...]
    return block.reshape(block.shape[0] * block.shape[2], block.shape[3])


def weight_specs(section, gate_up, down):
    fsdp = gate_up.shape[0] // 2
    at = lambda e: (section, e, 0, 0)
    return [
        pl.BlockSpec((fsdp, 1) + gate_up.shape[2:], at),
        pl.BlockSpec((fsdp, 1) + down.shape[2:], at),
    ]


def forward_body(width, last, x_ref, gate_up_ref, down_ref, *refs):
    if len(refs) == 4:
        incoming, out_ref, both_ref, total = refs
    else:
        incoming, (out_ref, both_ref, total) = None, refs
    e = pl.program_id(0)
    both = jnp.dot(x_ref[:, :width], merged(gate_up_ref), preferred_element_type=F32)
    both_ref[0] = both.astype(BF16)
    gate, up = both[:, :FF], both[:, FF:]
    weight = gate_of(x_ref[:, width:], lax.axis_index("expert") * (last + 1) + e)
    act = (gate * jax.nn.sigmoid(gate) * up * weight).astype(BF16)
    part = jnp.dot(act, merged(down_ref), preferred_element_type=F32)

    @pl.when(e == 0)
    def _():
        total[...] = part if incoming is None else part + incoming[...].astype(F32)

    @pl.when(e > 0)
    def _():
        total[...] += part

    @pl.when(e == last)
    def _():
        out_ref[...] = total[...].astype(out_ref.dtype)


def experts_forward(section, x_ext, gate_up, down, incoming, out_dtype):
    rows, wide = x_ext.shape
    count, columns = gate_up.shape[1], gate_up.shape[3]
    width = wide - LANES
    const = lambda e: (0, 0)
    each = lambda e: (e, 0, 0)
    in_specs = [
        pl.BlockSpec((rows, wide), const),
        *weight_specs(section, gate_up, down),
    ]
    operands = [x_ext, gate_up, down]
    if incoming is not None:
        in_specs.append(pl.BlockSpec((rows, width), const))
        operands.append(incoming)
    return pl.pallas_call(
        functools.partial(forward_body, width, count - 1),
        grid=(count,),
        in_specs=in_specs,
        out_specs=[pl.BlockSpec((rows, width), const), pl.BlockSpec((1, rows, columns), each)],
        out_shape=[
            jax.ShapeDtypeStruct((rows, width), out_dtype),
            jax.ShapeDtypeStruct((count, rows, columns), BF16),
        ],
        scratch_shapes=[pltpu.VMEM((rows, width), F32)],
        compiler_params=pltpu.CompilerParams(vmem_limit_bytes=40 * 2**20),
        cost_estimate=pl.CostEstimate(
            flops=2 * rows * count * width * (columns + FF),
            bytes_accessed=2 * count * width * (columns + FF) + 2 * rows * count * columns,
            transcendentals=rows * count * FF,
        ),
    )(*operands)


def backward_body(width, last, grad_ref, lanes_ref, both_ref, gate_up_ref, down_ref, *refs):
    if len(refs) == 5:
        incoming, out_ref, grad_both_ref, act_ref, total = refs
    else:
        incoming, (out_ref, grad_both_ref, act_ref, total) = None, refs
    e = pl.program_id(0)
    which = lax.axis_index("expert") * (last + 1) + e
    weight = gate_of(lanes_ref[...], which)
    grad = lax.dot_general(grad_ref[...], merged(down_ref), ACROSS, preferred_element_type=F32)
    gate = both_ref[0, :, :FF].astype(F32)
    up = both_ref[0, :, FF:].astype(F32)
    sigma = jax.nn.sigmoid(gate)
    silu = gate * sigma
    act = silu * up
    grad_weight = jnp.sum(grad * act, 1, keepdims=True)
    grad_act = grad * weight
    act_ref[0] = (act * weight).astype(BF16)
    grad_gate = grad_act * up * (sigma * (1.0 + gate * (1.0 - sigma)))
    grad_both = jnp.concatenate([grad_gate, grad_act * silu], 1).astype(BF16)
    grad_both_ref[0] = grad_both
    part = lax.dot_general(grad_both, merged(gate_up_ref), ACROSS, preferred_element_type=F32)
    high = grad_weight.astype(BF16).astype(F32)
    lane = lax.broadcasted_iota(jnp.int32, lanes_ref.shape, 1)
    extra = jnp.where(lane == which, high, jnp.where(lane == which + LOW, grad_weight - high, 0.0))

    @pl.when(e == 0)
    def _():
        if incoming is None:
            total[:, :width] = part
            total[:, width:] = extra
        else:
            total[:, :width] = part + incoming[:, :width].astype(F32)
            total[:, width:] = extra + incoming[:, width:].astype(F32)

    @pl.when(e > 0)
    def _():
        total[:, :width] += part
        total[:, width:] += extra

    @pl.when(e == last)
    def _():
        out_ref[...] = total[...].astype(out_ref.dtype)


def experts_backward(section, grad, x_ext, both, gate_up, down, incoming, out_dtype):
    rows, wide = x_ext.shape
    count, columns = gate_up.shape[1], gate_up.shape[3]
    width = wide - LANES
    const = lambda e: (0, 0)
    each = lambda e: (e, 0, 0)
    in_specs = [
        pl.BlockSpec((rows, width), const),
        pl.BlockSpec((rows, LANES), lambda e: (0, width // LANES)),
        pl.BlockSpec((1, rows, columns), each),
        *weight_specs(section, gate_up, down),
    ]
    operands = [grad, x_ext, both, gate_up, down]
    if incoming is not None:
        in_specs.append(pl.BlockSpec((rows, wide), const))
        operands.append(incoming)
    return pl.pallas_call(
        functools.partial(backward_body, width, count - 1),
        grid=(count,),
        in_specs=in_specs,
        out_specs=[
            pl.BlockSpec((rows, wide), const),
            pl.BlockSpec((1, rows, columns), each),
            pl.BlockSpec((1, rows, FF), each),
        ],
        out_shape=[
            jax.ShapeDtypeStruct((rows, wide), out_dtype),
            jax.ShapeDtypeStruct((count, rows, columns), BF16),
            jax.ShapeDtypeStruct((count, rows, FF), BF16),
        ],
        scratch_shapes=[pltpu.VMEM((rows, wide), F32)],
        compiler_params=pltpu.CompilerParams(vmem_limit_bytes=40 * 2**20),
        cost_estimate=pl.CostEstimate(
            flops=2 * rows * count * width * (columns + FF),
            bytes_accessed=2 * count * width * (columns + FF) + 5 * rows * count * columns,
            transcendentals=rows * count * FF,
        ),
    )(*operands)


def query_layout(segment, token_rows):
    n = lax.axis_size("expert")
    me = lax.axis_index("expert")
    offset = me * token_rows
    labels = jnp.arange(NCONT + 1, dtype=jnp.int32)
    member = (segment[:, None] == labels[None, :]).astype(jnp.int32)
    totals = jnp.sum(member, 0)
    starts = jnp.cumsum(totals) - totals
    query_seg = lax.dynamic_slice_in_dim(segment, offset, token_rows)
    query_idx = offset + jnp.arange(token_rows, dtype=jnp.int32)
    first = jnp.sum((query_seg[:, None] == labels[None, :]).astype(jnp.int32) * starts[None, :], 1)
    query_pos = jnp.where(query_seg == 0, query_idx, totals[0] + query_idx - first)
    parts = []
    for step in range(n):
        base = lax.rem(me - step + n, n) * token_rows
        key_seg = lax.dynamic_slice_in_dim(segment, base, token_rows)
        key_idx = base + jnp.arange(token_rows, dtype=jnp.int32)
        allowed = (key_idx[:, None] <= query_idx[None, :]) & (
            (key_seg[:, None] == 0) | (key_seg[:, None] == query_seg[None, :])
        )
        parts.append(jnp.where(allowed, 0.0, -1e30).astype(F32))
    half = HEAD_SIZE // 2
    freq = THETA ** (-jnp.arange(half, dtype=F32) / half)
    angle = query_pos.astype(F32)[:, None] * freq[None, :]
    cosine, sine = jnp.cos(angle), jnp.sin(angle)
    wide = jnp.concatenate([cosine] * 4, 1), jnp.concatenate([-sine, sine, -sine, sine], 1)
    return jnp.concatenate(parts, 0), wide, (cosine.T, sine.T)


PAIR = 2 * HEAD_SIZE
GROUP = QUERY_HEADS // KEY_VALUE_HEADS
FACTOR = HEAD_SIZE ** (-0.5)


def head(ref, index):
    return ref[..., index * HEAD_SIZE : (index + 1) * HEAD_SIZE]


def attend_body(q_ref, kv_ref, bias_ref, out_ref, lse_ref):
    lse = []
    outs = []
    for pair in range(2):
        keys, values = head(kv_ref[0], pair), head(kv_ref[1], pair)
        values_t = values.astype(F32).T.astype(BF16)
        for g in range(GROUP):
            queries = head(q_ref[...], pair * GROUP + g) * FACTOR
            scores = lax.dot_general(keys, queries, ACROSS, preferred_element_type=F32) + bias_ref[...]
            top = jnp.max(scores, 0, keepdims=True)
            weights = jnp.exp(scores - top)
            total = jnp.sum(weights, 0, keepdims=True)
            probs = (weights * (1.0 / total)).astype(BF16)
            outs.append(jnp.dot(values_t, probs, preferred_element_type=F32))
            lse.append(top + jnp.log(total))
    out_ref[...] = jnp.concatenate(outs, 0).T.astype(BF16)
    lse.append(jnp.zeros((2, lse[0].shape[1]), F32))
    lse_ref[0] = jnp.concatenate(lse, 0)


def attend(queries, kv, bias):
    rows = queries.shape[0]
    count = kv.shape[1]
    steps = KEY_VALUE_HEADS // 2
    wide = 2 * GROUP * HEAD_SIZE
    return pl.pallas_call(
        attend_body,
        grid=(steps,),
        in_specs=[
            pl.BlockSpec((rows, wide), lambda p: (0, p)),
            pl.BlockSpec((2, count, PAIR), lambda p: (0, 0, p)),
            pl.BlockSpec((count, rows), lambda p: (0, 0)),
        ],
        out_specs=[
            pl.BlockSpec((rows, wide), lambda p: (0, p)),
            pl.BlockSpec((1, 8, rows), lambda p: (p, 0, 0)),
        ],
        out_shape=[
            jax.ShapeDtypeStruct(queries.shape, BF16),
            jax.ShapeDtypeStruct((steps, 8, rows), F32),
        ],
        compiler_params=pltpu.CompilerParams(vmem_limit_bytes=40 * 2**20),
        cost_estimate=pl.CostEstimate(
            flops=16 * QUERY_HEADS * rows * count * HEAD_SIZE,
            bytes_accessed=8 * rows * QUERY_HEADS * HEAD_SIZE + 4 * kv.size,
            transcendentals=QUERY_HEADS * rows * count,
        ),
    )(queries, kv, bias)


def attend_back_body(q_ref, kv_ref, grad_ref, bias_ref, lse_ref, cos_ref, sin_ref, grad_q_ref, grad_kv_ref):
    half = HEAD_SIZE // 2
    cosine, sine = cos_ref[...], sin_ref[...]
    grad_q = []
    for pair in range(2):
        keys, values = head(kv_ref[0], pair), head(kv_ref[1], pair)
        keys_t = keys.astype(F32).T.astype(BF16)
        grad_keys, grad_values = None, None
        for g in range(GROUP):
            h = pair * GROUP + g
            queries = head(q_ref[...], h) * FACTOR
            grad = head(grad_ref[...], h)
            scores = lax.dot_general(keys, queries, ACROSS, preferred_element_type=F32) + bias_ref[...]
            probs = jnp.exp(scores - lse_ref[0, h : h + 1, :])
            grad_probs = lax.dot_general(values, grad, ACROSS, preferred_element_type=F32)
            product = probs * grad_probs
            inner = jnp.sum(product, 0, keepdims=True)
            grad_scores = (product - probs * inner).astype(BF16)
            dv = jnp.dot(probs.astype(BF16), grad, preferred_element_type=F32)
            dk = jnp.dot(grad_scores, queries, preferred_element_type=F32)
            grad_values = dv if grad_values is None else grad_values + dv
            grad_keys = dk if grad_keys is None else grad_keys + dk
            dq = jnp.dot(keys_t, grad_scores, preferred_element_type=F32) * FACTOR
            upper, lower = dq[:half], dq[half:]
            grad_q += [upper * cosine + lower * sine, lower * cosine - upper * sine]
        grad_kv_ref[0, :, pair * HEAD_SIZE : (pair + 1) * HEAD_SIZE] = grad_keys.astype(BF16)
        grad_kv_ref[1, :, pair * HEAD_SIZE : (pair + 1) * HEAD_SIZE] = grad_values.astype(BF16)
    grad_q_ref[...] = jnp.concatenate(grad_q, 0).T.astype(BF16)


def attend_back(queries, kv, grad, bias, lse, cosine_t, sine_t):
    rows = queries.shape[0]
    count = kv.shape[1]
    steps = KEY_VALUE_HEADS // 2
    wide = 2 * GROUP * HEAD_SIZE
    half = HEAD_SIZE // 2
    columns = pl.BlockSpec((rows, wide), lambda p: (0, p))
    pairs = pl.BlockSpec((2, count, PAIR), lambda p: (0, 0, p))
    table = pl.BlockSpec((half, rows), lambda p: (0, 0))
    return pl.pallas_call(
        attend_back_body,
        grid=(steps,),
        in_specs=[
            columns, pairs, columns,
            pl.BlockSpec((count, rows), lambda p: (0, 0)),
            pl.BlockSpec((1, 8, rows), lambda p: (p, 0, 0)),
            table, table,
        ],
        out_specs=[columns, pairs],
        out_shape=[
            jax.ShapeDtypeStruct(queries.shape, BF16),
            jax.ShapeDtypeStruct(kv.shape, BF16),
        ],
        compiler_params=pltpu.CompilerParams(vmem_limit_bytes=40 * 2**20),
        cost_estimate=pl.CostEstimate(
            flops=40 * QUERY_HEADS * rows * count * HEAD_SIZE,
            bytes_accessed=12 * rows * QUERY_HEADS * HEAD_SIZE + 8 * kv.size,
            transcendentals=QUERY_HEADS * rows * count,
        ),
    )(queries, kv, grad, bias, lse, cosine_t, sine_t)


def ring_of(block, axis="expert"):
    blocks = [block]
    for _ in range(lax.axis_size(axis) - 1):
        blocks.append(onward(blocks[-1], axis))
    return blocks


def up_line(block):
    n = lax.axis_size("expert")
    return lax.ppermute(block, "expert", [(i, i + 1) for i in range(n - 1)])


def down_line(block):
    n = lax.axis_size("expert")
    return lax.ppermute(block, "expert", [(i + 1, i) for i in range(n - 1)])


def attention_forward(x, layout, pieces, n_total):
    bias, tables, _ = layout
    normed, queries, own_kv, small, qkv = project(x, tables, pieces, n_total)
    ring = [own_kv]
    for _ in range(lax.axis_size("expert") - 1):
        ring.append(up_line(ring[-1]))
    kv = jnp.concatenate(ring, 1)
    attended, lse = attend(queries, kv, bias)
    return normed, queries, kv, small, qkv, attended, lse


def moe_forward(section, hidden, x_ext, gate_up, down):
    n = lax.axis_size("expert")
    ring_x = ring_of(x_ext)
    own, both = experts_forward(section, x_ext, gate_up, down, None, F32)
    ring_both = [both]
    arriving = None
    for step in range(1, n):
        part, both = experts_forward(section, ring_x[step], gate_up, down, arriving, BF16)
        ring_both.append(both)
        arriving = onward(part, "expert")
    result = hidden + own + arriving.astype(F32)
    return result.astype(BF16), ring_x, ring_both


def moe_backward(section, ring_grad, ring_x, ring_both, gate_up, down):
    n = lax.axis_size("expert")
    own, grad_both, act = experts_backward(
        section, ring_grad[0], ring_x[0], ring_both[0], gate_up, down, None, F32
    )
    ring_grad_both, ring_act = [grad_both], [act]
    arriving = None
    for step in range(1, n):
        part, grad_both, act = experts_backward(
            section, ring_grad[step], ring_x[step], ring_both[step], gate_up, down, arriving, BF16
        )
        ring_grad_both.append(grad_both)
        ring_act.append(act)
        arriving = onward(part, "expert")
    return own, arriving, ring_grad_both, ring_act


def down_body(n, *refs):
    grads, acts, out_ref, whole, turned_act = refs[:n], refs[n : 2 * n], refs[2 * n], refs[-2], refs[-1]
    rows = grads[0].shape[0]

    @pl.when(pl.program_id(0) == 0)
    def _():
        for t in range(n):
            whole[t * rows : (t + 1) * rows, :] = grads[t][...]

    for t in range(n):
        turned_act[:, t * rows : (t + 1) * rows] = acts[t][0].astype(F32).T.astype(BF16)
    step = 512
    for k in range(0, whole.shape[1], step):
        out_ref[0, :, k : k + step] = jnp.dot(
            turned_act[...], whole[:, k : k + step], preferred_element_type=F32
        ).astype(BF16)


def down_products(ring_grad, ring_act):
    n = len(ring_grad)
    rows, width = ring_grad[0].shape
    count = ring_act[0].shape[0]
    return pl.pallas_call(
        functools.partial(down_body, n),
        grid=(count,),
        in_specs=[pl.BlockSpec((rows, width), lambda e: (0, 0))] * n
        + [pl.BlockSpec((1, rows, FF), lambda e: (e, 0, 0))] * n,
        out_specs=pl.BlockSpec((1, FF, width), lambda e: (e, 0, 0)),
        out_shape=jax.ShapeDtypeStruct((count, FF, width), BF16),
        scratch_shapes=[pltpu.VMEM((n * rows, width), BF16), pltpu.VMEM((FF, n * rows), BF16)],
        compiler_params=pltpu.CompilerParams(vmem_limit_bytes=44 * 2**20),
        cost_estimate=pl.CostEstimate(
            flops=2 * n * rows * count * width * FF,
            bytes_accessed=2 * count * FF * (width + n * rows), transcendentals=0,
        ),
    )(*ring_grad, *ring_act)


def gate_up_body(n, *refs):
    exts, grads, out_ref, turned_x, whole = refs[:n], refs[n : 2 * n], refs[-3], refs[-2], refs[-1]
    rows = grads[0].shape[1]
    width = turned_x.shape[0]

    @pl.when(pl.program_id(0) == 0)
    def _():
        for t in range(n):
            turned_x[:, t * rows : (t + 1) * rows] = exts[t][:, :width].astype(F32).T.astype(BF16)

    for t in range(n):
        whole[t * rows : (t + 1) * rows, :] = grads[t][0]
    step = 256
    for k in range(0, whole.shape[1], step):
        out_ref[0, :, k : k + step] = jnp.dot(
            turned_x[...], whole[:, k : k + step], preferred_element_type=F32
        ).astype(BF16)


def gate_up_products(ring_x, ring_grad_both, first, count, others=()):
    n = len(ring_x)
    rows, wide = ring_x[0].shape
    width = wide - LANES
    columns = ring_grad_both[0].shape[2]
    return pl.pallas_call(
        functools.partial(gate_up_body, n),
        grid=(count,),
        in_specs=[pl.BlockSpec((rows, wide), lambda e: (0, 0))] * n
        + [pl.BlockSpec((1, rows, columns), lambda e: (first + e, 0, 0))] * n
        + [pl.BlockSpec(memory_space=pl.ANY)] * len(others),
        out_specs=pl.BlockSpec((1, width, columns), lambda e: (e, 0, 0)),
        out_shape=jax.ShapeDtypeStruct((count, width, columns), BF16),
        scratch_shapes=[pltpu.VMEM((width, n * rows), BF16), pltpu.VMEM((n * rows, columns), BF16)],
        compiler_params=pltpu.CompilerParams(vmem_limit_bytes=44 * 2**20),
        cost_estimate=pl.CostEstimate(
            flops=2 * n * rows * count * width * columns,
            bytes_accessed=2 * count * columns * (width + n * rows), transcendentals=0,
        ),
    )(*ring_x, *ring_grad_both, *others)


def expert_products(ring_grad, ring_x, ring_grad_both, ring_act):
    count = ring_act[0].shape[0]
    grad_down = down_products(ring_grad, ring_act)
    cut = (count + 1) // 2
    parts = [
        gate_up_products(ring_x, ring_grad_both, 0, cut, (grad_down,)),
        gate_up_products(ring_x, ring_grad_both, cut, count - cut, (grad_down,)),
    ]
    return [grad_down, *parts]


def attention_backward(queries, kv, grad_attended, lse, layout):
    bias, _, turned_tables = layout
    n = lax.axis_size("expert")
    rows = queries.shape[0]
    grad_q, grad_kv = attend_back(queries, kv, grad_attended, bias, lse, *turned_tables)
    arriving = None
    for step in range(1, n):
        place = n - step
        part = grad_kv[:, place * rows : (place + 1) * rows]
        if arriving is not None:
            part = add(part, arriving)
        arriving = down_line(part)
    return grad_q, grad_kv[:, :rows], arriving


def halves(block, bit):
    mine = (lax.axis_index("fsdp") // bit) % 2
    return pick(block, mine), pick(block, 1 - mine)


def add(a, b):
    return (a.astype(F32) + b.astype(F32)).astype(BF16)


def scatter_dense(keep, send):
    n = lax.axis_size("expert")
    me = lax.axis_index("expert")
    bits = bits_of("fsdp")
    highs, rows, columns = keep.shape
    block = add(keep, swap(send, "fsdp", 1)).reshape(highs, n, rows // n, columns)
    arriving = None
    for step in range(1, n):
        part = pick(block, lax.rem(me - step + n, n), 1)
        if arriving is not None:
            part = add(part, arriving)
        arriving = onward(part, "expert")
    block = add(pick(block, me, 1), arriving)
    for bit in bits[:-1]:
        block = block.reshape(2, -1, rows // n, columns)
        keep, send = halves(block, bit)
        block = add(keep, swap(send, "fsdp", bit))
    return block.reshape(rows // n, columns)


def scatter_expert(block):
    return lax.psum_scatter(block, "fsdp", scatter_dimension=1, tiled=True)


def toward(block, target):
    return lax.ppermute(block, "section", [(1 - target, target)])


def shards(
    x_in, cotangent, seg_ids, routes, query_key_value_weight, w_out, w_router,
    norm1_gain, norm2_gain, w_gate_up, w_down,
):
    section = lax.axis_index("section")
    first = section == 0
    n = lax.axis_size("expert")
    n_total = w_router.shape[-1]
    rows, width = x_in.shape[1:]
    qkv_columns = query_key_value_weight.shape[-1]

    def by_section(block):
        other = swap(block, "section", 1)
        return jnp.where(first, block, other), jnp.where(first, other, block)

    tokens = pick(x_in, section)
    cot = pick(cotangent, section)
    segment = pick(seg_ids, section)
    packed = jnp.concatenate(
        [
            query_key_value_weight[0], w_router[0], norm1_gain[0][:, None], norm2_gain[0][:, None],
            jnp.zeros((w_router.shape[1], LANES - n_total - 2), BF16),
        ], 1,
    )
    packed = by_section(packed)
    outs = by_section(w_out[0])
    peer_route = swap(pick(routes[0], 1 - section), "section", 1)
    own_route = pick(routes[0], section)
    route = (jnp.where(first, own_route, peer_route), jnp.where(first, peer_route, own_route))
    layout = query_layout(segment, rows)
    down = lax.all_gather(w_down[0], ("section", "fsdp"), axis=0)
    gate_up = lax.all_gather(w_gate_up[0], ("section", "fsdp"), axis=0)

    qkv_pieces = Pieces(dense_pieces(packed[0], False))
    out_pieces = Pieces(dense_pieces(outs[0], True))
    normed0, q0, kv0, small0, qkv0, attended0, lse0 = attention_forward(
        tokens, layout, qkv_pieces, n_total
    )
    hidden0, ext0, wout0 = route_tokens(tokens, attended0, small0, route[0], out_pieces, n_total)
    ring_cot = ring_of(tie(cot, q0))
    ext0 = tie(ext0, *ring_cot)
    qkv_pieces = Pieces(dense_pieces(tie(packed[1], ext0), False))
    out_pieces = Pieces(dense_pieces(tie(outs[1], ext0), False))
    out0, ring_x0, both0 = moe_forward(0, hidden0, ext0, gate_up, down)

    normed1, q1, kv1, small1, qkv1, attended1, lse1 = attention_forward(
        out0, layout, qkv_pieces, n_total
    )
    hidden1, ext1, wout1 = route_tokens(out0, attended1, small1, route[1], out_pieces, n_total)
    out1, ring_x1, both1 = moe_forward(1, hidden1, ext1, gate_up, down)

    def backward(s, ring_grad, ring_x, both, hidden, small, wout, x, normed, q, kv, lse, qkv, attended, earlier):
        own, arriving, grad_both, act = moe_backward(s, ring_grad, ring_x, both, gate_up, down)
        products = expert_products(ring_grad, ring_x, grad_both, act)
        scattered = [scatter_expert(p) for p in products]
        grad_hidden, grad_attn, grad_attended, grad_logits, gain_two = route_back(
            own, arriving, hidden, ring_x[0], ring_grad[0], small, wout, n_total
        )
        grad_out = dense_product(attended, grad_attn)
        if earlier:
            lse = tie(lse, *earlier)
        grad_q, own_kv, arriving_kv = attention_backward(q, kv, grad_attended, lse, layout)
        grad_mixed, grad_x, gain_one = project_back(
            grad_q, own_kv, arriving_kv, layout[1], x, grad_hidden, small, qkv, n_total
        )
        grad_packed = dense_product(
            normed, grad_mixed, n_total, (ring_x[0][:, :width], grad_logits, gain_one, gain_two)
        )
        dense = [scatter_dense(*grad_out), scatter_dense(*grad_packed)]
        return grad_x, scattered + dense

    grad1, owned1 = backward(
        1, ring_cot, ring_x1, both1, hidden1, small1, wout1, out0, normed1, q1, kv1, lse1, qkv1, attended1, ()
    )
    sent1 = [toward(b, 1) for b in owned1]
    grad0, owned0 = backward(
        0, ring_of(grad1), ring_x0, both0, hidden0, small0, wout0, tokens, normed0, q0, kv0, lse0, qkv0,
        attended0, sent1,
    )
    sent0 = [toward(b, 0) for b in owned0]

    def exchanged(a0, a1):
        mine, other = jnp.where(first, a0, a1), swap(jnp.where(first, a1, a0), "section", 1)
        return jnp.stack([jnp.where(first, mine, other), jnp.where(first, other, mine)])[None]

    section_out = exchanged(out0, out1)
    in_grad = exchanged(grad0, grad1)

    grads = [
        jnp.where(first, b0, b1).astype(F32) + jnp.where(first, r0, r1).astype(F32)
        for b0, b1, r0, r1 in zip(owned0, owned1, sent0, sent1)
    ]
    grad_down, gate_up_low, gate_up_high, grad_w_out, grad_packed = grads
    grad_gate_up = jnp.concatenate([gate_up_low, gate_up_high], 0)
    return (
        section_out,
        in_grad,
        grad_packed[:, :qkv_columns][None],
        grad_w_out[None],
        grad_packed[:, qkv_columns : qkv_columns + n_total][None],
        grad_packed[:, qkv_columns + n_total][None],
        grad_packed[:, qkv_columns + n_total + 1][None],
        grad_gate_up[None],
        grad_down[None],
    )


def solution(mesh):
    both = ("fsdp", "expert")
    weights = (
        P("section", both, None),
        P("section", both, None),
        P("section", both, None),
        P("section", both),
        P("section", both),
        P("section", "expert", "fsdp", None),
        P("section", "expert", "fsdp", None),
    )
    return jax.shard_map(
        shards,
        mesh=mesh,
        in_specs=(
            P(None, both, None),
            P(None, both, None),
            P(None, "fsdp"),
            P("section", None, both, None),
        )
        + weights,
        out_specs=(P("section", None, both, None), P("section", None, both, None)) + weights,
        check_vma=False,
    )
```

```python
import functools

import jax
import jax.numpy as jnp
from jax import lax
from jax.experimental import pallas as pl
from jax.experimental.pallas import tpu as pltpu
from jax.sharding import PartitionSpec as P

QUERY_HEADS = 24
KEY_VALUE_HEADS = 8
HEAD_SIZE = 64
FF = 512
NCONT = 8
EPS = 1e-06
THETA = 10000.0
LANES = 128
LOW = 64

F32 = jnp.float32
BF16 = jnp.bfloat16
ACROSS = (((1,), (1,)), ((), ()))
MESH = pl.DeviceIdType.MESH


def lasting(micros):
    return pl.CostEstimate(
        flops=int(micros * 1.1e9), bytes_accessed=int(micros * 3.6e6), transcendentals=0
    )


PAIR = 2 * HEAD_SIZE
GROUP = QUERY_HEADS // KEY_VALUE_HEADS
FACTOR = HEAD_SIZE ** (-0.5)


def swap(block, axis, bit):
    return lax.ppermute(block, axis, [(i, i ^ bit) for i in range(lax.axis_size(axis))])


def onward(block, axis):
    n = lax.axis_size(axis)
    return lax.ppermute(block, axis, [(i, (i + 1) % n) for i in range(n)])


def bits_of(axis):
    bits, bit = [], lax.axis_size(axis) // 2
    while bit:
        bits.append(bit)
        bit //= 2
    return bits


def pick(block, index, axis=0):
    return lax.dynamic_index_in_dim(block, index, axis, keepdims=False)


def after(block, *others):
    return lax.optimization_barrier((block, *others))[0]


def head(block, index):
    return block[..., index * HEAD_SIZE : (index + 1) * HEAD_SIZE]


def tie(block, *others):
    def body(*refs):
        pass

    return pl.pallas_call(
        body,
        out_shape=jax.ShapeDtypeStruct(block.shape, block.dtype),
        in_specs=[pl.BlockSpec(memory_space=pl.ANY)] * (1 + len(others)),
        out_specs=pl.BlockSpec(memory_space=pl.ANY),
        input_output_aliases={0: 0},
        cost_estimate=lasting(0.004),
    )(block, *others)


def peers():
    n = lax.axis_size("expert")
    me, fsdp, section = lax.axis_index("expert"), lax.axis_index("fsdp"), lax.axis_index("section")
    return (
        [{"expert": lax.rem(me + step, n)} for step in range(1, n)]
        + [{"fsdp": fsdp ^ bit} for bit in bits_of("fsdp")[:-1]]
        + [{"section": 1 - section}]
    )


def meet():
    barrier = pltpu.get_barrier_semaphore()
    others = peers()
    for other in others:
        pl.semaphore_signal(barrier, inc=1, device_id=other, device_id_type=MESH)
    pl.semaphore_wait(barrier, len(others))


class Rides:
    def __init__(self, rides):
        self.rides = rides
        self.count = len(rides)
        self.blocks = [b for b, _, _ in rides]
        self.specs = [pl.BlockSpec(memory_space=pltpu.HBM)] * self.count
        self.shapes = [jax.ShapeDtypeStruct(b.shape, b.dtype) for b in self.blocks]
        self.scratch = [pltpu.SemaphoreType.DMA((2, self.count))] if rides else []

    def copies(self, refs, outs, sems):
        n = lax.axis_size("expert")
        me, fsdp, section = lax.axis_index("expert"), lax.axis_index("fsdp"), lax.axis_index("section")
        made = []
        for k, (_, axis, where) in enumerate(self.rides):
            target = {
                "expert": lambda: lax.rem(me + where, n),
                "fsdp": lambda: fsdp ^ where,
                "section": lambda: 1 - section,
            }[axis]()
            copy = pltpu.make_async_remote_copy(
                src_ref=refs[k], dst_ref=outs[k], send_sem=sems.at[0, k], recv_sem=sems.at[1, k],
                device_id={axis: target}, device_id_type=MESH,
            )
            sends = receives = None
            if axis == "section" and where is not None:
                sends, receives = section != where, section == where
            made.append((copy, sends, receives))
        return made

    @staticmethod
    def when(condition, act):
        if condition is None:
            act()
        else:
            pl.when(condition)(act)

    def start(self, refs, outs, sems):
        for copy, sends, _ in self.copies(refs, outs, sems):
            self.when(sends, copy.start)

    def finish(self, refs, outs, sems):
        for copy, sends, receives in self.copies(refs, outs, sems):
            self.when(sends, copy.wait_send)
            self.when(receives, copy.wait_recv)


def dense_pieces(block, y_first, wait=None):
    n = lax.axis_size("expert")
    bits = bits_of("fsdp")
    early, late = (bits[:-1], bits[-1:]) if y_first else ([], bits)
    held = [(0, block)]
    for bit in early:
        held += [(mask ^ bit, swap(b, "fsdp", bit)) for mask, b in held]
    pieces = [(mask, 0, b) for mask, b in held]
    moving = held
    for step in range(1, n):
        moving = [(mask, onward(b, "expert")) for mask, b in moving]
        pieces += [(mask, step, b) for mask, b in moving]
    if wait is not None:
        mask, step, b = pieces[-1]
        pieces[-1] = (mask, step, tie(b, wait))
    for bit in late:
        pieces += [(mask ^ bit, step, swap(b, "fsdp", bit)) for mask, step, b in pieces]
    rows, columns = block.shape
    if rows % 16 == 0:
        return pieces
    whole = jnp.zeros((lax.axis_size("fsdp") * n * rows, columns), block.dtype)
    fsdp, expert = lax.axis_index("fsdp"), lax.axis_index("expert")
    for mask, step, b in pieces:
        start = ((fsdp ^ mask) * n + lax.rem(expert - step + n, n)) * rows
        whole = lax.dynamic_update_slice_in_dim(whole, b, start, 0)
    return [(0, 0, whole)]


class Pieces:
    def __init__(self, pieces):
        self.spots = [(mask, step) for mask, step, _ in pieces]
        self.blocks = [b for _, _, b in pieces]
        self.rows, self.columns = self.blocks[0].shape
        self.count = len(self.blocks)

    def copies(self, refs, whole, sems):
        n = lax.axis_size("expert")
        fsdp, expert = lax.axis_index("fsdp"), lax.axis_index("expert")
        out = []
        for k, (mask, step) in enumerate(self.spots):
            if self.count == 1:
                out.append(pltpu.make_async_copy(refs[k], whole, sems.at[k]))
                continue
            start = ((fsdp ^ mask) * n + lax.rem(expert - step + n, n)) * self.rows
            rows = pl.ds(pl.multiple_of(start, self.rows), self.rows)
            out.append(pltpu.make_async_copy(refs[k], whole.at[rows, :], sems.at[k]))
        return out


def vmem_call(body, out_shape, operands, anywhere, scratch_shapes=(), any_out=0, flops=0):
    vmem = pl.BlockSpec(memory_space=pltpu.VMEM)
    hbm = pl.BlockSpec(memory_space=pl.ANY)
    size = sum(o.size * o.dtype.itemsize for o in operands)
    return pl.pallas_call(
        body,
        out_shape=out_shape,
        in_specs=[vmem] * (len(operands) - anywhere) + [hbm] * anywhere,
        out_specs=[vmem] * (len(out_shape) - any_out) + [hbm] * any_out,
        scratch_shapes=list(scratch_shapes),
        compiler_params=pltpu.CompilerParams(vmem_limit_bytes=44 * 2**20),
        cost_estimate=lasting(0.1),
    )(*operands)


def turned(block, cosine, sine):
    half = HEAD_SIZE // 2
    wide = block.shape[1]
    lane = lax.broadcasted_iota(jnp.int32, block.shape, 1)
    partner = jnp.where(
        lane % HEAD_SIZE < half, pltpu.roll(block, wide - half, 1), pltpu.roll(block, half, 1)
    )
    return block * cosine + partner * sine


def attend_pair(queries, keys, values, bias):
    lse, outs = [], []
    for pair in range(2):
        own_keys, own_values = head(keys, pair), head(values, pair)
        values_t = own_values.astype(F32).T.astype(BF16)
        for g in range(GROUP):
            own_queries = head(queries, pair * GROUP + g) * FACTOR
            scores = lax.dot_general(own_keys, own_queries, ACROSS, preferred_element_type=F32) + bias
            top = jnp.max(scores, 0, keepdims=True)
            weights = jnp.exp(scores - top)
            total = jnp.sum(weights, 0, keepdims=True)
            probs = (weights * (1.0 / total)).astype(BF16)
            outs.append(jnp.dot(values_t, probs, preferred_element_type=F32))
            lse.append(top + jnp.log(total))
    lse.append(jnp.zeros((8 - len(lse), lse[0].shape[1]), F32))
    return jnp.concatenate(outs, 0).T.astype(BF16), jnp.concatenate(lse, 0)


def attention_body(pieces, n_total, x_ref, cos_ref, sin_ref, bias_ref, *refs):
    weights, refs = refs[: pieces.count], refs[pieces.count :]
    normed_ref, q_ref, kv_ref, small_ref, attended_ref, lse_ref, out_ref = refs[:7]
    whole, sems, out_sem, send_sems, recv_sems = refs[7:]
    n = lax.axis_size("expert")
    me = lax.axis_index("expert")
    rows = x_ref.shape[0]
    pairs = kv_ref.shape[0]

    barrier = pltpu.get_barrier_semaphore()

    @pl.when(me > 0)
    def _():
        pl.semaphore_signal(barrier, inc=1, device_id={"expert": me - 1}, device_id_type=MESH)

    copies = pieces.copies(weights, whole, sems)
    for copy in copies:
        copy.start()
    x = x_ref[...].astype(F32)
    scaled = x * lax.rsqrt(jnp.mean(x * x, -1, keepdims=True) + EPS)
    for copy in copies:
        copy.wait()
    back = pltpu.make_async_copy(whole, out_ref, out_sem)
    back.start()
    columns = pieces.columns - LANES
    small = whole[:, columns:].astype(F32).T
    small_ref[...] = small
    normed = (scaled * small[n_total : n_total + 1, :]).astype(BF16)
    normed_ref[...] = normed
    block = KEY_VALUE_HEADS * HEAD_SIZE
    repeat = block // cos_ref.shape[1]
    cosine = jnp.concatenate([cos_ref[...]] * repeat, 1)
    sine = jnp.concatenate([sin_ref[...]] * repeat, 1)
    count = columns // block

    def columns_of(k):
        return jnp.dot(normed, whole[:, k * block : (k + 1) * block], preferred_element_type=F32)

    keys = turned(columns_of(count - 2), cosine, sine).astype(BF16)
    values = columns_of(count - 1).astype(BF16)
    for p in range(pairs):
        kv_ref[p, 0, 0] = keys[:, p * PAIR : (p + 1) * PAIR]
        kv_ref[p, 0, 1] = values[:, p * PAIR : (p + 1) * PAIR]

        for t in range(1, n):

            @pl.when(me < t)
            def _():
                kv_ref[p, t] = jnp.zeros(kv_ref.shape[2:], BF16)

    def hop(p, t):
        return pltpu.make_async_remote_copy(
            src_ref=kv_ref.at[p, t], dst_ref=kv_ref.at[p, t + 1], send_sem=send_sems.at[p, t],
            recv_sem=recv_sems.at[p, t], device_id={"expert": me + 1}, device_id_type=MESH,
        )

    def forward_step(p, t):
        if t > 0:

            @pl.when(me >= t)
            def _():
                hop(p, t - 1).wait_recv()

        if t < n - 1:

            @pl.when((me < n - 1) & (me >= t))
            def _():
                hop(p, t).start()

    @pl.when(me < n - 1)
    def _():
        pl.semaphore_wait(barrier, 1)

    for p in range(pairs):
        forward_step(p, 0)
    for k in range(count - 2):
        q_ref[:, k * block : (k + 1) * block] = turned(columns_of(k), cosine, sine).astype(BF16)
    for t in range(1, n - 1):
        for p in range(pairs):
            forward_step(p, t)
    wide = 2 * GROUP * HEAD_SIZE

    def one(p, carry):
        forward_step(p, n - 1)
        spot = pl.ds(pl.multiple_of(p * wide, LANES), wide)
        pair = kv_ref[p]
        attended, lse = attend_pair(
            q_ref[:, spot], pair[:, 0].reshape(n * rows, PAIR), pair[:, 1].reshape(n * rows, PAIR),
            bias_ref[...],
        )
        attended_ref[:, spot] = attended
        lse_ref[p] = lse
        return carry

    lax.fori_loop(0, pairs, one, 0)
    for t in range(n - 1):

        @pl.when((me < n - 1) & (me >= t))
        def _():
            for p in range(pairs):
                hop(p, t).wait_send()

    back.wait()


def attention_forward(x, layout, pieces, n_total):
    bias, tables, _ = layout
    n = lax.axis_size("expert")
    rows, width = x.shape
    columns = pieces.columns
    pairs = KEY_VALUE_HEADS // 2
    vmem, hbm = pl.BlockSpec(memory_space=pltpu.VMEM), pl.BlockSpec(memory_space=pl.ANY)
    struct = jax.ShapeDtypeStruct
    dma = pltpu.SemaphoreType.DMA
    heads = QUERY_HEADS * HEAD_SIZE
    return pl.pallas_call(
        functools.partial(attention_body, pieces, n_total),
        in_specs=[vmem] * 4 + [hbm] * pieces.count,
        out_specs=[vmem] * 6 + [hbm],
        out_shape=[
            struct((rows, width), BF16),
            struct((rows, heads), BF16),
            struct((pairs, n, 2, rows, PAIR), BF16),
            struct((LANES, width), F32),
            struct((rows, heads), BF16),
            struct((pairs, 8, rows), F32),
            struct((width, columns), BF16),
        ],
        scratch_shapes=[
            pltpu.VMEM((width, columns), BF16), dma((pieces.count,)), dma,
            dma((pairs, n - 1)), dma((pairs, n - 1)),
        ],
        compiler_params=pltpu.CompilerParams(
            vmem_limit_bytes=48 * 2**20, has_side_effects=True, collective_id=4
        ),
        cost_estimate=lasting(0.64),
    )(x, *tables, bias, *pieces.blocks)


def route_body(pieces, n_total, x_ref, attended_ref, small_ref, route_ref, *refs):
    weights, refs = refs[: pieces.count], refs[pieces.count :]
    hidden_ref, ext_ref, out_ref, whole, sems, out_sem = refs
    copies = pieces.copies(weights, whole, sems)
    for copy in copies:
        copy.start()
    for copy in copies:
        copy.wait()
    back = pltpu.make_async_copy(whole, out_ref, out_sem)
    back.start()
    rows, width = x_ref.shape
    block = 512
    for k in range(0, width, block):
        hidden_ref[:, k : k + block] = x_ref[:, k : k + block].astype(F32) + jnp.dot(
            attended_ref[...], whole[:, k : k + block], preferred_element_type=F32
        )
    hidden = hidden_ref[...]
    scale = lax.rsqrt(jnp.mean(hidden * hidden, -1, keepdims=True) + EPS)
    normed = (hidden * scale * small_ref[n_total + 1 : n_total + 2, :]).astype(BF16)
    ext_ref[:, :width] = normed
    logits = lax.dot_general(
        normed, small_ref[...].astype(BF16), ACROSS, preferred_element_type=F32
    )
    lane = lax.broadcasted_iota(jnp.int32, logits.shape, 1)
    chosen = lane == route_ref[:, 0:1]
    for k in range(1, route_ref.shape[1]):
        chosen = chosen | (lane == route_ref[:, k : k + 1])
    logits = jnp.where(chosen, logits, -1e30)
    weights = jnp.where(chosen, jnp.exp(logits - jnp.max(logits, 1, keepdims=True)), 0.0)
    gates = weights / jnp.sum(weights, 1, keepdims=True)
    high = gates.astype(BF16).astype(F32)
    ext_ref[:, width:] = (high + pltpu.roll(gates - high, LOW, 1)).astype(BF16)
    back.wait()


def route_tokens(x, attended, small, route, pieces, n_total):
    rows, width = x.shape
    return vmem_call(
        functools.partial(route_body, pieces, n_total),
        [
            jax.ShapeDtypeStruct((rows, width), F32),
            jax.ShapeDtypeStruct((rows, width + LANES), BF16),
            jax.ShapeDtypeStruct((width, pieces.columns), BF16),
        ],
        [x, attended, small, route, *pieces.blocks],
        pieces.count,
        [
            pltpu.VMEM((width, pieces.columns), BF16),
            pltpu.SemaphoreType.DMA((pieces.count,)),
            pltpu.SemaphoreType.DMA,
        ],
        1,
        2 * rows * width * pieces.columns,
    )


def joined(lanes):
    lane = lax.broadcasted_iota(jnp.int32, lanes.shape, 1)
    return jnp.where(lane < LOW, lanes + pltpu.roll(lanes, LOW, 1), 0.0)


def route_back_body(
    n_total, summed_ref, hidden_ref, lanes_ref, grad_ref, small_ref, weight_ref,
    grad_hidden_ref, grad_attn_ref, grad_attended_ref, grad_logits_ref, gain_ref,
):
    rows, width = hidden_ref.shape
    gates = joined(lanes_ref[:, width:].astype(F32))
    grad_gates = joined(summed_ref[:, width:])
    grad_logits = gates * (grad_gates - jnp.sum(gates * grad_gates, 1, keepdims=True))
    grad_logits = grad_logits.astype(BF16)
    grad_logits_ref[...] = grad_logits
    grad_normed = (
        summed_ref[:, :width]
        + jnp.dot(grad_logits, small_ref[...].astype(BF16), preferred_element_type=F32)
    )
    hidden = hidden_ref[...]
    scale = lax.rsqrt(jnp.mean(hidden * hidden, -1, keepdims=True) + EPS)
    unit = hidden * scale
    gain = jnp.sum(grad_normed * unit, 0, keepdims=True)
    gain_ref[...] = jnp.broadcast_to(gain, gain_ref.shape)
    lifted = grad_normed * small_ref[n_total + 1 : n_total + 2, :]
    grad_hidden = (
        grad_ref[...].astype(F32)
        + scale * lifted
        - unit * (scale * jnp.mean(lifted * unit, -1, keepdims=True))
    )
    grad_hidden_ref[...] = grad_hidden
    grad_attn = grad_hidden.astype(BF16)
    grad_attn_ref[...] = grad_attn
    block = 512
    for k in range(0, width, block):
        grad_attended_ref[:, k : k + block] = lax.dot_general(
            grad_attn, weight_ref[k : k + block, :], ACROSS, preferred_element_type=F32
        ).astype(BF16)


def route_back(summed, hidden, x_ext, grad, small, weight, n_total):
    rows, width = hidden.shape
    return vmem_call(
        functools.partial(route_back_body, n_total),
        [
            jax.ShapeDtypeStruct((rows, width), F32),
            jax.ShapeDtypeStruct((rows, width), BF16),
            jax.ShapeDtypeStruct((rows, weight.shape[0]), BF16),
            jax.ShapeDtypeStruct((rows, LANES), BF16),
            jax.ShapeDtypeStruct((8, width), F32),
        ],
        [summed, hidden, x_ext, grad, small, weight],
        0,
        flops=2 * rows * width * width,
    )


def project_back_body(
    n_total, columns, grad_q_ref, grad_kv_ref, cos_ref, sin_ref, x_ref, grad_hidden_ref, small_ref,
    weight_ref, grad_mixed_ref, grad_x_ref, gain_ref,
):
    rows, width = x_ref.shape
    block = KEY_VALUE_HEADS * HEAD_SIZE
    repeat = block // cos_ref.shape[1]
    cosine = jnp.concatenate([cos_ref[...]] * repeat, 1)
    sine = jnp.concatenate([sin_ref[...]] * repeat, 1)
    pairs = grad_kv_ref.shape[0]
    grad_keys = jnp.concatenate([grad_kv_ref[p, 0] for p in range(pairs)], 1)
    grad_values = jnp.concatenate([grad_kv_ref[p, 1] for p in range(pairs)], 1)
    query_columns = columns - 2 * block
    grad_mixed_ref[:, :query_columns] = grad_q_ref[...]
    grad_mixed_ref[:, query_columns : query_columns + block] = turned(grad_keys, cosine, -sine).astype(BF16)
    grad_mixed_ref[:, query_columns + block :] = grad_values.astype(BF16)
    grad_mixed = grad_mixed_ref[...]
    parts = []
    step = 512
    for k in range(0, width, step):
        parts.append(
            lax.dot_general(
                grad_mixed, weight_ref[k : k + step, :columns], ACROSS, preferred_element_type=F32
            )
        )
    grad_normed = jnp.concatenate(parts, 1)
    x = x_ref[...].astype(F32)
    scale = lax.rsqrt(jnp.mean(x * x, -1, keepdims=True) + EPS)
    unit = x * scale
    gain = jnp.sum(grad_normed * unit, 0, keepdims=True)
    gain_ref[...] = jnp.broadcast_to(gain, gain_ref.shape)
    lifted = grad_normed * small_ref[n_total : n_total + 1, :]
    grad_x_ref[...] = (
        grad_hidden_ref[...]
        + scale * lifted
        - unit * (scale * jnp.mean(lifted * unit, -1, keepdims=True))
    ).astype(BF16)


def project_back(grad_q, grad_kv, tables, x, grad_hidden, small, weight, n_total):
    rows, width = x.shape
    columns = weight.shape[1] - LANES
    return vmem_call(
        functools.partial(project_back_body, n_total, columns),
        [
            jax.ShapeDtypeStruct((rows, columns), BF16),
            jax.ShapeDtypeStruct((rows, width), BF16),
            jax.ShapeDtypeStruct((8, width), F32),
        ],
        [grad_q, grad_kv, *tables, x, grad_hidden, small, weight],
        0,
        flops=2 * rows * width * columns,
    )


def product_body(
    extra, left_ref, right_ref, normed_ref, logits_ref, gain_one_ref, gain_two_ref, left_two_ref, right_two_ref,
    out_ref, blocks, send_sems, recv_sems,
):
    highs, rows = out_ref.shape[0], out_ref.shape[1]
    columns = right_ref.shape[1]
    fsdp = lax.axis_index("fsdp")
    core = fsdp % 2
    other = fsdp + 1 - 2 * core
    barrier = pltpu.get_barrier_semaphore()
    pl.semaphore_signal(barrier, inc=1, device_id={"fsdp": other}, device_id_type=MESH)

    def send(high):
        return pltpu.make_async_remote_copy(
            src_ref=blocks.at[0, high], dst_ref=blocks.at[1, high], send_sem=send_sems.at[high],
            recv_sem=recv_sems.at[high], device_id={"fsdp": other}, device_id_type=MESH,
        )

    def products(high, whose):
        spot = pl.ds(pl.multiple_of((high * 2 + whose) * rows, LANES), rows)

        def turned_rows(ref):
            return ref[:, spot].astype(F32).T.astype(BF16)

        step = 512
        left = turned_rows(left_ref)
        for k in range(0, columns, step):
            yield k, step, jnp.dot(left, right_ref[:, k : k + step], preferred_element_type=F32)
        small = jnp.dot(turned_rows(normed_ref), logits_ref[...], preferred_element_type=F32)
        lane = lax.broadcasted_iota(jnp.int32, small.shape, 1)
        one = gain_one_ref[:, spot].T[:, 0:1]
        two = gain_two_ref[:, spot].T[:, 0:1]
        yield columns, LANES, jnp.where(lane == extra, one, jnp.where(lane == extra + 1, two, small))
        left = turned_rows(left_two_ref)
        for k in range(0, right_two_ref.shape[1], step):
            yield columns + LANES + k, step, jnp.dot(
                left, right_two_ref[:, k : k + step], preferred_element_type=F32
            )

    for high in range(highs):
        for start, size, value in products(high, 1 - core):
            blocks[0, high, :, start : start + size] = value.astype(BF16)
        if high == 0:
            pl.semaphore_wait(barrier, 1)
        send(high).start()
    for high in range(highs):
        send(high).wait_recv()
        for start, size, value in products(high, core):
            arrived = blocks[1, high, :, start : start + size].astype(F32)
            out_ref[high, :, start : start + size] = (value + arrived).astype(BF16)
    for high in range(highs):
        send(high).wait_send()


def dense_product(left, right, extra, small, second):
    tokens, width = left.shape
    highs = lax.axis_size("fsdp") // 2
    rows = width // (2 * highs)
    columns = right.shape[1] + LANES + second[1].shape[1]
    vmem = pl.BlockSpec(memory_space=pltpu.VMEM)
    operands = [left, right, *small, *second]
    return pl.pallas_call(
        functools.partial(product_body, extra),
        in_specs=[vmem] * len(operands),
        out_specs=vmem,
        out_shape=jax.ShapeDtypeStruct((highs, rows, columns), BF16),
        scratch_shapes=[
            pltpu.VMEM((2, highs, rows, columns), BF16),
            pltpu.SemaphoreType.DMA((highs,)),
            pltpu.SemaphoreType.DMA((highs,)),
        ],
        compiler_params=pltpu.CompilerParams(
            vmem_limit_bytes=48 * 2**20, has_side_effects=True, collective_id=6
        ),
        cost_estimate=lasting(0.3),
    )(*operands)


def experts_body(mode, section, rides, extra, *refs):
    forward, backward = mode != "backward", mode != "forward"
    refs = list(refs)
    take = lambda count: [refs.pop(0) for _ in range(count)]
    if mode == "backward":
        moving_ref, ext_ref, both_in = take(3)
        grads_ref = None
    else:
        (moving_ref,) = take(1)
        grads_ref = take(1)[0] if mode == "both" else None
    gate_up_ref, down_ref = take(2)
    riding = take(rides.count)
    take(extra)
    out_ref, ring_out = take(2)
    if mode == "forward":
        (both_out,) = take(1)
    else:
        grad_both_out, act_out = take(2)
        parts_out = take(1)[0] if mode == "both" else None
    arrived = take(rides.count)
    gate_up, down, weight_sems, ring, ring_sems, out_sems = take(6)
    sums, sum_sems, total = take(3)
    if mode == "forward":
        stage, stage_sems = take(2)
    else:
        stage, act_stage, stage_sems = take(3)
        if mode == "both":
            part_total, part_stage, part_sems = take(3)
        else:
            lanes, lane_sem, both_stage, both_sems = take(4)

    n = lax.axis_size("expert")
    me = lax.axis_index("expert")
    right, left = lax.rem(me + 1, n), lax.rem(me + n - 1, n)
    experts, fsdp = gate_up.shape[0], gate_up.shape[1]
    rows = moving_ref.shape[0]
    width = down.shape[3]

    if rides.count:
        ride_sems = refs.pop()
        meet()
        rides.start(riding, arrived, ride_sems)
    else:
        barrier = pltpu.get_barrier_semaphore()
        pl.semaphore_signal(barrier, inc=1, device_id={"expert": left}, device_id_type=MESH)

    loads = []
    for e in range(experts):
        of = pl.ds(section * fsdp, fsdp)
        loads.append(
            [
                pltpu.make_async_copy(gate_up_ref.at[of, e], gate_up.at[e], weight_sems.at[0, e]),
                pltpu.make_async_copy(down_ref.at[of, e], down.at[e], weight_sems.at[1, e]),
            ]
        )
        for load in loads[-1]:
            load.start()
    if mode == "backward":
        fetch = lambda k: pltpu.make_async_copy(
            both_in.at[k // experts, k % experts], both_stage.at[k % 2], both_sems.at[k % 2]
        )
        fetch(0).start()
        lane_copy = pltpu.make_async_copy(ext_ref.at[:, :, pl.ds(width, LANES)], lanes, lane_sem)
        lane_copy.start()
    ring[0] = moving_ref[...]
    if not rides.count:
        pl.semaphore_wait(barrier, 1)

    hops = [
        pltpu.make_async_remote_copy(
            src_ref=ring.at[t], dst_ref=ring.at[t + 1], send_sem=ring_sems.at[0, t],
            recv_sem=ring_sems.at[1, t], device_id={"expert": right}, device_id_type=MESH,
        )
        for t in range(n - 1)
    ]
    carries = [
        pltpu.make_async_remote_copy(
            src_ref=sums.at[0, t], dst_ref=sums.at[1, t], send_sem=sum_sems.at[0, t],
            recv_sem=sum_sems.at[1, t], device_id={"expert": right}, device_id_type=MESH,
        )
        for t in range(n - 1)
    ]
    stores = [pltpu.make_async_copy(ring.at[t], ring_out.at[t], out_sems.at[t]) for t in range(n)]
    if mode == "backward":
        lane_copy.wait()

    for t in range(n):
        if t > 0:
            hops[t - 1].wait_recv()
        if t < n - 1:
            hops[t].start()
        stores[t].start()
        total[...] = jnp.zeros_like(total)
        if mode == "both":
            part_total[...] = jnp.zeros_like(part_total)

        def one(e, carry):
            k = t * experts + e
            slot = lax.rem(k, 2)
            which = me * experts + e
            weights_one = gate_up[e].reshape(fsdp * gate_up.shape[2], gate_up.shape[3])
            weights_two = down[e].reshape(fsdp * down.shape[2], width)
            if mode == "backward":
                weight = gate_of(lanes[t], which)
                fetch(k).wait()

                @pl.when(k + 1 < n * experts)
                def _():
                    pltpu.make_async_copy(
                        both_in.at[lax.div(k + 1, experts), lax.rem(k + 1, experts)],
                        both_stage.at[1 - slot], both_sems.at[1 - slot],
                    ).start()

                gate = both_stage[slot, :, :FF].astype(F32)
                up = both_stage[slot, :, FF:].astype(F32)
            else:
                weight = gate_of(ring[t, :, width:], which)
                both = jnp.dot(ring[t, :, :width], weights_one, preferred_element_type=F32)
                gate, up = both[:, :FF], both[:, FF:]
            sigma = jax.nn.sigmoid(gate)
            silu = gate * sigma
            act = silu * up
            gated = (act * weight).astype(BF16)
            if forward:
                part = jnp.dot(gated, weights_two, preferred_element_type=F32)
                if mode == "forward":
                    total[...] += part
                else:
                    part_total[...] += part

            if mode == "forward":

                @pl.when(k >= 2)
                def _():
                    pltpu.make_async_copy(stage.at[slot], both_out.at[t, e], stage_sems.at[slot]).wait()

                stage[slot] = both.astype(BF16)
                pltpu.make_async_copy(stage.at[slot], both_out.at[t, e], stage_sems.at[slot]).start()
            else:
                grad_rows = ring[t] if mode == "backward" else grads_ref[t]
                grad = lax.dot_general(grad_rows, weights_two, ACROSS, preferred_element_type=F32)
                grad_weight = jnp.sum(grad * act, 1, keepdims=True)
                grad_act = grad * weight
                grad_gate = grad_act * up * (sigma * (1.0 + gate * (1.0 - sigma)))
                grad_both = jnp.concatenate([grad_gate, grad_act * silu], 1).astype(BF16)
                total[:, :width] += lax.dot_general(
                    grad_both, weights_one, ACROSS, preferred_element_type=F32
                )
                high = grad_weight.astype(BF16).astype(F32)
                lane = lax.broadcasted_iota(jnp.int32, (rows, LANES), 1)
                total[:, width:] += jnp.where(
                    lane == which, high, jnp.where(lane == which + LOW, grad_weight - high, 0.0)
                )

                @pl.when(k >= 2)
                def _():
                    pltpu.make_async_copy(
                        stage.at[slot], grad_both_out.at[t, e], stage_sems.at[0, slot]
                    ).wait()
                    pltpu.make_async_copy(
                        act_stage.at[slot], act_out.at[t, e], stage_sems.at[1, slot]
                    ).wait()

                stage[slot] = grad_both
                act_stage[slot] = gated
                pltpu.make_async_copy(stage.at[slot], grad_both_out.at[t, e], stage_sems.at[0, slot]).start()
                pltpu.make_async_copy(act_stage.at[slot], act_out.at[t, e], stage_sems.at[1, slot]).start()
            return carry

        if t == 0:
            for e in range(experts):
                for load in loads[e]:
                    load.wait()
                one(e, 0)
        else:
            lax.fori_loop(0, experts, one, 0)

        if mode == "both":
            if t >= 2:
                pltpu.make_async_copy(part_stage.at[t % 2], parts_out.at[t - 2], part_sems.at[t % 2]).wait()
            part_stage[t % 2] = part_total[...].astype(BF16)
            pltpu.make_async_copy(part_stage.at[t % 2], parts_out.at[t], part_sems.at[t % 2]).start()
        if t == 0:
            out_ref[...] = total[...]
        else:
            if t > 1:
                carries[t - 2].wait_recv()
                sums[0, t - 1] = (total[...] + sums[1, t - 2].astype(F32)).astype(BF16)
            else:
                sums[0, 0] = total[...].astype(BF16)
            carries[t - 1].start()

    carries[n - 2].wait_recv()
    out_ref[...] += sums[1, n - 2].astype(F32)
    for t in range(n - 1):
        hops[t].wait_send()
        carries[t].wait_send()
    for store in stores:
        store.wait()
    last = n * experts - 1
    for k in (last - 1, last):
        t, e, slot = k // experts, k % experts, k % 2
        if mode == "forward":
            pltpu.make_async_copy(stage.at[slot], both_out.at[t, e], stage_sems.at[slot]).wait()
        else:
            pltpu.make_async_copy(stage.at[slot], grad_both_out.at[t, e], stage_sems.at[0, slot]).wait()
            pltpu.make_async_copy(act_stage.at[slot], act_out.at[t, e], stage_sems.at[1, slot]).wait()
    if mode == "both":
        for t in (n - 2, n - 1):
            pltpu.make_async_copy(part_stage.at[t % 2], parts_out.at[t], part_sems.at[t % 2]).wait()


def gate_of(lanes, which):
    place_of = lax.broadcasted_iota(jnp.int32, lanes.shape, 1)
    chosen = (place_of == which) | (place_of == which + LOW)
    return jnp.sum(jnp.where(chosen, lanes.astype(F32), 0.0), 1, keepdims=True)


def run_experts(mode, section, moving, inputs, gate_up, down, others=(), rides=()):
    rides = Rides(rides)
    n = lax.axis_size("expert")
    fsdp, experts = gate_up.shape[0] // 2, gate_up.shape[1]
    columns, width = gate_up.shape[3], down.shape[3]
    rows = moving.shape[0]
    wide = width + LANES
    vmem, hbm = pl.BlockSpec(memory_space=pltpu.VMEM), pl.BlockSpec(memory_space=pl.ANY)
    struct = jax.ShapeDtypeStruct
    dma = pltpu.SemaphoreType.DMA
    sum_wide = width if mode == "forward" else wide
    out_shape = [struct((rows, sum_wide), F32), struct((n,) + moving.shape, BF16)]
    scratch = [
        pltpu.VMEM((experts, fsdp) + gate_up.shape[2:], BF16),
        pltpu.VMEM((experts, fsdp) + down.shape[2:], BF16),
        dma((2, experts)),
        pltpu.VMEM((n,) + moving.shape, BF16),
        dma((2, n - 1)),
        dma((n,)),
        pltpu.VMEM((2, n - 1, rows, sum_wide), BF16),
        dma((2, n - 1)),
        pltpu.VMEM((rows, sum_wide), F32),
    ]
    if mode == "forward":
        out_shape += [struct((n, experts, rows, columns), BF16)]
        scratch += [pltpu.VMEM((2, rows, columns), BF16), dma((2,))]
    else:
        out_shape += [struct((n, experts, rows, columns), BF16), struct((n, experts, rows, FF), BF16)]
        scratch += [pltpu.VMEM((2, rows, columns), BF16), pltpu.VMEM((2, rows, FF), BF16), dma((2, 2))]
        if mode == "both":
            out_shape += [struct((n, rows, width), BF16)]
            scratch += [pltpu.VMEM((rows, width), F32), pltpu.VMEM((2, rows, width), BF16), dma((2,))]
        else:
            scratch += [
                pltpu.VMEM((n, rows, LANES), BF16), dma, pltpu.VMEM((2, rows, columns), BF16), dma((2,)),
            ]
    in_spec = {"forward": [vmem], "both": [vmem, vmem], "backward": [vmem, hbm, hbm]}[mode]
    products = {"forward": 1, "both": 2, "backward": 1}[mode]
    return pl.pallas_call(
        functools.partial(experts_body, mode, section, rides, len(others)),
        in_specs=in_spec + [hbm] * 2 + rides.specs + [hbm] * len(others),
        out_specs=[vmem] + [hbm] * (len(out_shape) - 1) + rides.specs,
        out_shape=out_shape + rides.shapes,
        scratch_shapes=scratch + rides.scratch,
        compiler_params=pltpu.CompilerParams(
            vmem_limit_bytes=56 * 2**20,
            has_side_effects=True,
            collective_id={"forward": 1, "both": 2, "backward": 3}[mode],
        ),
        cost_estimate=lasting(2.3),
    )(moving, *inputs, gate_up, down, *rides.blocks, *others)


def query_layout(segment, token_rows):
    n = lax.axis_size("expert")
    me = lax.axis_index("expert")
    offset = me * token_rows
    labels = jnp.arange(NCONT + 1, dtype=jnp.int32)
    member = (segment[:, None] == labels[None, :]).astype(jnp.int32)
    totals = jnp.sum(member, 0)
    starts = jnp.cumsum(totals) - totals
    query_seg = lax.dynamic_slice_in_dim(segment, offset, token_rows)
    query_idx = offset + jnp.arange(token_rows, dtype=jnp.int32)
    first = jnp.sum((query_seg[:, None] == labels[None, :]).astype(jnp.int32) * starts[None, :], 1)
    query_pos = jnp.where(query_seg == 0, query_idx, totals[0] + query_idx - first)
    parts = []
    for step in range(n):
        base = lax.rem(me - step + n, n) * token_rows
        key_seg = lax.dynamic_slice_in_dim(segment, base, token_rows)
        key_idx = base + jnp.arange(token_rows, dtype=jnp.int32)
        allowed = (key_idx[:, None] <= query_idx[None, :]) & (
            (key_seg[:, None] == 0) | (key_seg[:, None] == query_seg[None, :])
        )
        parts.append(jnp.where(allowed, 0.0, -1e30).astype(F32))
    half = HEAD_SIZE // 2
    freq = THETA ** (-jnp.arange(half, dtype=F32) / half)
    angle = query_pos.astype(F32)[:, None] * freq[None, :]
    cosine, sine = jnp.cos(angle), jnp.sin(angle)
    wide = jnp.concatenate([cosine] * 4, 1), jnp.concatenate([-sine, sine, -sine, sine], 1)
    return jnp.concatenate(parts, 0), wide, (cosine.T, sine.T)


def attention_back_body(rides, q_ref, kv_ref, grad_ref, bias_ref, lse_ref, cos_ref, sin_ref, *refs):
    riding, refs = refs[: rides.count], refs[rides.count :]
    grad_q_ref, out_ref = refs[:2]
    landed, refs = refs[2 : 2 + rides.count], refs[2 + rides.count :]
    parts, sums, send_sems, recv_sems = refs[:4]
    n = lax.axis_size("expert")
    me = lax.axis_index("expert")
    pairs, _, _, rows, _ = kv_ref.shape
    half = HEAD_SIZE // 2
    wide = 2 * GROUP * HEAD_SIZE
    if rides.count:
        meet()
        rides.start(riding, landed, refs[4])
    else:
        barrier = pltpu.get_barrier_semaphore()

        @pl.when(me < n - 1)
        def _():
            pl.semaphore_signal(barrier, inc=1, device_id={"expert": me + 1}, device_id_type=MESH)

    @pl.when(me == n - 1)
    def _():
        sums[1] = jnp.zeros(sums.shape[1:], BF16)

    def send(p, step):
        return pltpu.make_async_remote_copy(
            src_ref=sums.at[0, p, step - 1], dst_ref=sums.at[1, p, step - 1],
            send_sem=send_sems.at[p, step - 1], recv_sem=recv_sems.at[p, step - 1],
            device_id={"expert": me - 1}, device_id_type=MESH,
        )

    def arrived(p, step):
        @pl.when(me < n - 1)
        def _():
            send(p, step).wait_recv()

        return sums[1, p, step - 1].astype(F32)

    def move(p, step):
        value = parts[p, n - step]
        if step > 1:
            value = value + arrived(p, step - 1)
        if step == n:
            out_ref[p] = value
        else:
            sums[0, p, step - 1] = value.astype(BF16)

            @pl.when(me > 0)
            def _():
                send(p, step).start()

    def compute(p):
        cosine, sine = cos_ref[...], sin_ref[...]
        spot = pl.ds(pl.multiple_of(p * wide, LANES), wide)
        queries_all, grads_all = q_ref[:, spot], grad_ref[:, spot]
        block = kv_ref[p]
        keys_all, values_all = block[:, 0].reshape(n * rows, PAIR), block[:, 1].reshape(n * rows, PAIR)
        grad_q = []
        for pair in range(2):
            keys, values = head(keys_all, pair), head(values_all, pair)
            keys_t = keys.astype(F32).T.astype(BF16)
            grad_keys, grad_values = None, None
            for g in range(GROUP):
                h = pair * GROUP + g
                queries = head(queries_all, h) * FACTOR
                grad = head(grads_all, h)
                scores = lax.dot_general(keys, queries, ACROSS, preferred_element_type=F32) + bias_ref[...]
                probs = jnp.exp(scores - lse_ref[p, h : h + 1, :])
                grad_probs = lax.dot_general(values, grad, ACROSS, preferred_element_type=F32)
                product = probs * grad_probs
                inner = jnp.sum(product, 0, keepdims=True)
                grad_scores = (product - probs * inner).astype(BF16)
                dv = jnp.dot(probs.astype(BF16), grad, preferred_element_type=F32)
                dk = jnp.dot(grad_scores, queries, preferred_element_type=F32)
                grad_values = dv if grad_values is None else grad_values + dv
                grad_keys = dk if grad_keys is None else grad_keys + dk
                dq = jnp.dot(keys_t, grad_scores, preferred_element_type=F32) * FACTOR
                upper, lower = dq[:half], dq[half:]
                grad_q += [upper * cosine + lower * sine, lower * cosine - upper * sine]
            lanes = slice(pair * HEAD_SIZE, (pair + 1) * HEAD_SIZE)
            for t in range(n):
                parts[p, t, 0, :, lanes] = grad_keys[t * rows : (t + 1) * rows]
                parts[p, t, 1, :, lanes] = grad_values[t * rows : (t + 1) * rows]
        grad_q_ref[:, spot] = jnp.concatenate(grad_q, 0).T.astype(BF16)

    compute(0)
    if not rides.count:

        @pl.when(me > 0)
        def _():
            pl.semaphore_wait(barrier, 1)

    move(0, 1)

    def one(p, carry):
        compute(p)
        move(p, 1)
        for step in range(2, n + 1):

            @pl.when(p >= step - 1)
            def _():
                move(p - (step - 1), step)

        return carry

    lax.fori_loop(1, pairs, one, 0)
    for late in range(pairs, pairs + n - 1):
        for step in range(2, n + 1):
            if 0 <= late - (step - 1) < pairs:
                move(late - (step - 1), step)

    @pl.when(me > 0)
    def _():
        for p in range(pairs):
            for step in range(1, n):
                send(p, step).wait_send()

    if rides.count:
        rides.finish(riding, landed, refs[4])


def attention_backward(queries, kv, grad, lse, layout, rides=(), identity=5):
    bias, _, turned_tables = layout
    rides = Rides(rides)
    pairs, n, _, rows, _ = kv.shape
    vmem = pl.BlockSpec(memory_space=pltpu.VMEM)
    dma = pltpu.SemaphoreType.DMA
    out = pl.pallas_call(
        functools.partial(attention_back_body, rides),
        in_specs=[vmem] * 7 + rides.specs,
        out_specs=[vmem] * 2 + rides.specs,
        out_shape=[
            jax.ShapeDtypeStruct(queries.shape, BF16),
            jax.ShapeDtypeStruct((pairs, 2, rows, PAIR), F32),
        ]
        + rides.shapes,
        scratch_shapes=[
            pltpu.VMEM((pairs, n, 2, rows, PAIR), F32),
            pltpu.VMEM((2, pairs, n - 1, 2, rows, PAIR), BF16),
            dma((pairs, n - 1)),
            dma((pairs, n - 1)),
        ]
        + rides.scratch,
        compiler_params=pltpu.CompilerParams(
            vmem_limit_bytes=48 * 2**20, has_side_effects=True, collective_id=identity
        ),
        cost_estimate=lasting(0.9),
    )(queries, kv, grad, bias, lse, *turned_tables, *rides.blocks)
    return out[0], out[1], out[2:]


def ring_of(block, axis="expert"):
    blocks = [block]
    for _ in range(lax.axis_size(axis) - 1):
        blocks.append(onward(blocks[-1], axis))
    return blocks


def down_body(grads_ref, acts_ref, *refs):
    out_ref, turned_act = refs[-2], refs[-1]
    n, rows, width = grads_ref.shape
    for t in range(n):
        turned_act[:, t * rows : (t + 1) * rows] = acts_ref[t, 0].astype(F32).T.astype(BF16)
    step = 512
    for k in range(0, width, step):
        out_ref[0, :, k : k + step] = jnp.dot(
            turned_act[...], grads_ref[:, :, k : k + step].reshape(n * rows, step),
            preferred_element_type=F32,
        ).astype(BF16)


def down_products(grads, acts, others=()):
    n, rows, width = grads.shape
    count = acts.shape[1]
    return pl.pallas_call(
        down_body,
        grid=(count,),
        in_specs=[
            pl.BlockSpec((n, rows, width), lambda e: (0, 0, 0)),
            pl.BlockSpec((n, 1, rows, FF), lambda e: (0, e, 0, 0)),
        ]
        + [pl.BlockSpec(memory_space=pl.ANY)] * len(others),
        out_specs=pl.BlockSpec((1, FF, width), lambda e: (e, 0, 0)),
        out_shape=jax.ShapeDtypeStruct((count, FF, width), BF16),
        scratch_shapes=[pltpu.VMEM((FF, n * rows), BF16)],
        compiler_params=pltpu.CompilerParams(vmem_limit_bytes=44 * 2**20),
        cost_estimate=lasting(0.22),
    )(grads, acts, *others)


def gate_up_body(rides, exts_ref, grads_ref, *refs):
    riding, refs = refs[: rides.count], refs[len(refs) - rides.count - 4 :]
    low_ref, high_ref, arrived, sems, turned_x = refs[0], refs[1], refs[2 : 2 + rides.count], refs[-2], refs[-1]
    e = pl.program_id(0)
    n, _, rows, columns = grads_ref.shape
    width = turned_x.shape[0]
    cut = (pl.num_programs(0) + 1) // 2

    @pl.when(e == 0)
    def _():
        meet()
        rides.start(riding, arrived, sems)
        for t in range(n):
            turned_x[:, t * rows : (t + 1) * rows] = exts_ref[t, :, :width].astype(F32).T.astype(BF16)

    def fill(out_ref):
        step = 256
        for k in range(0, columns, step):
            out_ref[0, :, k : k + step] = jnp.dot(
                turned_x[...], grads_ref[:, 0, :, k : k + step].reshape(n * rows, step),
                preferred_element_type=F32,
            ).astype(BF16)

    @pl.when(e < cut)
    def _():
        fill(low_ref)

    @pl.when(e >= cut)
    def _():
        fill(high_ref)

    @pl.when(e == pl.num_programs(0) - 1)
    def _():
        rides.finish(riding, arrived, sems)


def gate_up_products(exts, grads, rides, identity, others=()):
    rides = Rides(rides)
    n, rows, wide = exts.shape
    width = wide - LANES
    count, columns = grads.shape[1], grads.shape[3]
    cut = (count + 1) // 2
    hbm = pl.BlockSpec(memory_space=pl.ANY)
    out = pl.pallas_call(
        functools.partial(gate_up_body, rides),
        grid=(count,),
        in_specs=[
            pl.BlockSpec((n, rows, wide), lambda e: (0, 0, 0)),
            pl.BlockSpec((n, 1, rows, columns), lambda e: (0, e, 0, 0)),
        ]
        + rides.specs
        + [hbm] * len(others),
        out_specs=[
            pl.BlockSpec((1, width, columns), lambda e: (jnp.minimum(e, cut - 1), 0, 0)),
            pl.BlockSpec((1, width, columns), lambda e: (jnp.maximum(e - cut, 0), 0, 0)),
        ]
        + rides.specs,
        out_shape=[
            jax.ShapeDtypeStruct((cut, width, columns), BF16),
            jax.ShapeDtypeStruct((count - cut, width, columns), BF16),
        ]
        + rides.shapes,
        scratch_shapes=rides.scratch + [pltpu.VMEM((width, n * rows), BF16)],
        compiler_params=pltpu.CompilerParams(
            vmem_limit_bytes=44 * 2**20, has_side_effects=True, collective_id=identity
        ),
        cost_estimate=lasting(0.24),
    )(exts, grads, *rides.blocks, *others)
    return out[:2], out[2:]


def add(a, b):
    return (a.astype(F32) + b.astype(F32)).astype(BF16)


def one_of(block, index, dim):
    return lax.dynamic_slice_in_dim(block, index, 1, dim)


def opened(block):
    highs, rows, columns = block.shape
    n = lax.axis_size("expert")
    return block.reshape([2] * (len(bits_of("fsdp")) - 1) + [n, 2, rows // n // 2, columns])


ORDERS = ["yzx", "zyx"]


def owned_body(rides, cuts, *refs):
    bits = bits_of("fsdp")[:-1]
    n = lax.axis_size("expert")
    me, section, fsdp = lax.axis_index("expert"), lax.axis_index("section"), lax.axis_index("fsdp")
    axes = [("y", bit) for bit in bits] + [("z", None), ("x", None)]
    own = [(fsdp // bit) % 2 for bit in bits] + [me, section]
    orders = ORDERS
    block_ref, riding, refs = refs[0], refs[1 : 1 + rides.count], refs[1 + rides.count :]
    out_ref, arrived, refs = refs[0], refs[1 : 1 + rides.count], list(refs[1 + rides.count :])
    if rides.count:
        ride_sems = refs.pop(0)
    sems, refs = refs[0], refs[1:]
    meet()
    if rides.count:
        rides.start(riding, arrived, ride_sems)
    used = [0]

    def steps(part):
        current, landing = refs[part][0], refs[part][1:]
        done, made = set(), []
        slot = 0
        for letter in orders[part]:
            for dim, (name, bit) in enumerate(axes):
                if name != letter:
                    continue
                size = n if name == "z" else 2

                def region(index, dim=dim, finished=frozenset(done)):
                    return tuple(
                        index if d == dim else (own[d] if d in finished else slice(None))
                        for d in range(len(axes))
                    )

                copies = []
                for step in range(1, size):
                    if name == "z":
                        there = lax.rem(me + step, n)
                        device = {"expert": there}
                    elif name == "y":
                        there, device = 1 - own[dim], {"fsdp": fsdp ^ bit}
                    else:
                        there, device = 1 - section, {"section": 1 - section}
                    copies.append(
                        pltpu.make_async_remote_copy(
                            src_ref=current.at[region(there)], dst_ref=landing[slot],
                            send_sem=sems.at[0, used[0]], recv_sem=sems.at[1, used[0]],
                            device_id=device, device_id_type=MESH,
                        )
                    )
                    used[0] += 1
                    slot += 1

                def start(copies=copies):
                    for copy in copies:
                        copy.start()

                def finish(copies=copies, region=region, dim=dim, spots=range(slot - len(copies), slot)):
                    spot = region(own[dim])
                    total = current[spot].astype(F32)
                    for copy, k in zip(copies, spots):
                        copy.wait_recv()
                        total = total + landing[k][...].astype(F32)
                    for copy in copies:
                        copy.wait_send()
                    current[spot] = total.astype(BF16)

                made.append((start, finish))
                done.add(dim)
        return made

    plans = []
    for part, (low, high) in enumerate(cuts):
        refs[part][0][...] = block_ref[..., low:high]
        plans.append(steps(part))
        plans[-1][0][0]()
    for stage in range(len(plans[0])):
        for plan in plans:
            plan[stage][1]()
            if stage + 1 < len(plan):
                plan[stage + 1][0]()
    for part, (low, high) in enumerate(cuts):
        out_ref[:, low:high] = refs[part][0][tuple(own)]
    if rides.count:
        rides.finish(riding, arrived, ride_sems)


def owned_rows(block, rides, identity):
    rides = Rides(rides)
    bits = len(bits_of("fsdp")) - 1
    n = lax.axis_size("expert")
    rows, columns = block.shape[-2:]
    much = columns // LANES * 3 // 5 * LANES
    cuts = [(0, much), (much, columns)]
    scratch = [pltpu.SemaphoreType.DMA((2, len(cuts) * (bits + n)))]
    for (low, high), order in zip(cuts, ORDERS):
        shape = list(block.shape[:-1]) + [high - low]
        buffers = [pltpu.VMEM(tuple(shape), BF16)]
        for letter in order:
            for dim, name in enumerate(["y"] * bits + ["z", "x"]):
                if name == letter:
                    size = shape[dim]
                    shape[dim] = 0
                    landing = tuple(v for v in shape if v)
                    buffers += [pltpu.VMEM(landing, BF16)] * (size - 1)
        scratch.append(buffers)
    out = pl.pallas_call(
        functools.partial(owned_body, rides, cuts),
        in_specs=[pl.BlockSpec(memory_space=pltpu.VMEM)] + rides.specs,
        out_specs=[pl.BlockSpec(memory_space=pltpu.VMEM)] + rides.specs,
        out_shape=[jax.ShapeDtypeStruct((rows, columns), BF16)] + rides.shapes,
        scratch_shapes=rides.scratch + scratch,
        compiler_params=pltpu.CompilerParams(
            vmem_limit_bytes=48 * 2**20, has_side_effects=True, collective_id=identity
        ),
        cost_estimate=lasting(0.24),
    )(block, *rides.blocks)
    return out[0], out[1:]


def scatter_expert(block):
    return lax.psum_scatter(block, "fsdp", scatter_dimension=1, tiled=True)


def toward(block, target):
    return lax.ppermute(block, "section", [(1 - target, target)])


def shards(
    x_in, cotangent, seg_ids, routes, query_key_value_weight, w_out, w_router,
    norm1_gain, norm2_gain, w_gate_up, w_down,
):
    section = lax.axis_index("section")
    first = section == 0
    n = lax.axis_size("expert")
    n_total = w_router.shape[-1]
    rows, width = x_in.shape[1:]
    qkv_columns = query_key_value_weight.shape[-1]

    def by_section(block):
        other = swap(block, "section", 1)
        return jnp.where(first, block, other), jnp.where(first, other, block)

    tokens = pick(x_in, section)
    cot = pick(cotangent, section)
    segment = pick(seg_ids, section)
    packed = jnp.concatenate(
        [
            query_key_value_weight[0], w_router[0], norm1_gain[0][:, None], norm2_gain[0][:, None],
            jnp.zeros((w_router.shape[1], LANES - n_total - 2), BF16),
        ], 1,
    )
    packed = by_section(packed)
    outs = by_section(w_out[0])
    peer_route = swap(pick(routes[0], 1 - section), "section", 1)
    own_route = pick(routes[0], section)
    route = (jnp.where(first, own_route, peer_route), jnp.where(first, peer_route, own_route))
    layout = query_layout(segment, rows)
    down = lax.all_gather(w_down[0], ("section", "fsdp"), axis=0)
    gate_up = lax.all_gather(w_gate_up[0], ("section", "fsdp"), axis=0)

    qkv_pieces = Pieces(dense_pieces(packed[0], True))
    normed0, q0, kv0, small0, attended0, lse0, qkv0 = attention_forward(
        tokens, layout, qkv_pieces, n_total
    )
    out_pieces = Pieces(dense_pieces(outs[0], True, lse0))
    hidden0, ext0, wout0 = route_tokens(tokens, attended0, small0, route[0], out_pieces, n_total)
    qkv_pieces = Pieces(dense_pieces(tie(packed[1], q0), True))
    ring_cot = ring_of(tie(cot, lse0))
    next_pieces = Pieces(dense_pieces(tie(outs[1], q0), True))
    summed, ring_x0, both0 = run_experts(
        "forward", 0, ext0, (), gate_up, down, (ring_cot[-1], *qkv_pieces.blocks, *next_pieces.blocks)
    )
    out0 = (hidden0 + summed).astype(BF16)

    normed1, q1, kv1, small1, attended1, lse1, qkv1 = attention_forward(
        out0, layout, qkv_pieces, n_total
    )
    out_pieces = next_pieces
    hidden1, ext1, wout1 = route_tokens(out0, attended1, small1, route[1], out_pieces, n_total)
    grads1 = jnp.stack(ring_cot)
    summed, ring_x1, grad_both, act, parts = run_experts("both", 1, ext1, (grads1,), gate_up, down)

    grad_down = down_products(grads1, act)
    high_parts = [(parts[step], "expert", n - step) for step in range(1, n) if step != n // 2]
    (low, high), come = gate_up_products(
        ring_x1, grad_both, high_parts + [(out0, "section", 0)], 7, (grad_down,)
    )
    come, sent_out0 = come[:-1], come[-1]
    products1 = [grad_down, low, high]
    experts1 = [scatter_expert(p) for p in products1]
    grad_hidden, grad_attn, grad_attended, grad_logits1, gain_two1 = route_back(
        summed, tie(hidden1, *products1), ext1, cot, small1, wout1, n_total
    )
    grad_q, grad_kv, _ = attention_backward(q1, kv1, grad_attended, lse1, layout)
    grad_mixed1, grad1, gain_one1 = project_back(
        grad_q, grad_kv, layout[1], out0, grad_hidden, small1, qkv1, n_total
    )
    sum1 = opened(
        dense_product(
            normed1, grad_mixed1, n_total, (ext1, grad_logits1, gain_one1, gain_two1), (attended1, grad_attn)
        )
    )

    x_dim = sum1.ndim - 3
    crossing = one_of(sum1, 1 - section, x_dim)
    summed, grads0, grad_both, act = run_experts(
        "backward", 0, grad1, (ring_x0, both0), gate_up, down, (crossing,)
    )
    sum1 = add(one_of(sum1, section, x_dim), swap(crossing, "section", 1))
    grad_down = down_products(grads0, act, (sum1, *experts1))
    y_rides, fsdp = [], lax.axis_index("fsdp")
    bits = bits_of("fsdp")[:-1]
    if len(bits) == 1:
        mine = (fsdp // bits[0]) % 2
        y_rides = [(one_of(sum1, 1 - mine, 0), "fsdp", bits[0])]
    (low, high), crossed = gate_up_products(
        ring_x0, grad_both,
        [(parts[n // 2], "expert", n - n // 2), (experts1[2], "section", 1), (grad1, "section", 1)] + y_rides,
        8, (grad_down,),
    )
    middle, sent_high1, sent_grad1 = crossed[:3]
    if y_rides:
        sum1 = add(one_of(sum1, mine, 0), crossed[3])
    else:
        for dim, bit in enumerate(bits):
            mine = (fsdp // bit) % 2
            sum1 = add(one_of(sum1, mine, dim), swap(one_of(sum1, 1 - mine, dim), "fsdp", bit))
    products0 = [grad_down, low, high]
    experts0 = [scatter_expert(grad_down), scatter_expert(low)]
    experts0.append(scatter_expert(tie(high, experts0[0])))
    out1 = hidden1 + parts[0].astype(F32) + middle.astype(F32)
    for part in come:
        out1 = out1 + part.astype(F32)
    out1 = out1.astype(BF16)
    grad_hidden, grad_attn, grad_attended, grad_logits0, gain_two0 = route_back(
        summed, tie(hidden0, *products0), ext0, grad1, small0, wout0, n_total
    )
    me, z_dim = lax.axis_index("expert"), sum1.ndim - 4
    z_rides = [
        (one_of(sum1, lax.rem(me + step, n), z_dim), "expert", step) for step in range(1, n)
    ]
    grad_q, grad_kv, crossed = attention_backward(
        q0, kv0, grad_attended, lse0, layout, z_rides + [(experts1[0], "section", 1)], 9
    )
    half1 = one_of(sum1, me, z_dim).astype(F32)
    for part in crossed[: n - 1]:
        half1 = half1 + part.astype(F32)
    half1 = half1.astype(BF16).reshape(half1.shape[-2:])
    sent_down1 = crossed[n - 1]
    grad_mixed0, grad0, gain_one0 = project_back(
        grad_q, grad_kv, layout[1], tokens, grad_hidden, small0, qkv0, n_total
    )
    sum0 = opened(
        dense_product(
            normed0, grad_mixed0, n_total, (ext0, grad_logits0, gain_one0, gain_two0),
            (attended0, grad_attn),
        )
    )
    half0, crossed = owned_rows(
        sum0,
        (
            (experts0[0], "section", 0), (experts0[1], "section", 0), (grad0, "section", 0),
            (experts1[1], "section", 1), (half1, "section", 1), (out1, "section", 1),
        ),
        10,
    )
    sent_down0, sent_low0, sent_grad0, sent_low1, sent_half1, sent_out1 = crossed
    sent0 = [sent_down0, sent_low0, toward(experts0[2], 0)]
    sent1 = [sent_down1, sent_low1, sent_high1]

    def stacked(a0, a1, came0, came1):
        mine, other = jnp.where(first, a0, a1), jnp.where(first, came0, came1)
        return jnp.stack([jnp.where(first, mine, other), jnp.where(first, other, mine)])[None]

    section_out = stacked(out0, out1, sent_out0, sent_out1)
    in_grad = stacked(grad0, grad1, sent_grad0, sent_grad1)
    grad_down, gate_up_low, gate_up_high = [
        jnp.where(first, b0, b1).astype(F32) + jnp.where(first, r0, r1).astype(F32)
        for b0, b1, r0, r1 in zip(experts0, experts1, sent0, sent1)
    ]
    other = jnp.where(first, toward(half0, 0), sent_half1).astype(F32)
    own = jnp.where(first, half0, half1).astype(F32)
    grad_dense = jnp.concatenate([jnp.where(first, own, other), jnp.where(first, other, own)], 0)
    grad_packed, grad_w_out = grad_dense[:, : qkv_columns + LANES], grad_dense[:, qkv_columns + LANES :]
    grad_gate_up = jnp.concatenate([gate_up_low, gate_up_high], 0)
    return (
        section_out,
        in_grad,
        grad_packed[:, :qkv_columns][None],
        grad_w_out[None],
        grad_packed[:, qkv_columns : qkv_columns + n_total][None],
        grad_packed[:, qkv_columns + n_total][None],
        grad_packed[:, qkv_columns + n_total + 1][None],
        grad_gate_up[None],
        grad_down[None],
    )


def solution(mesh):
    both = ("fsdp", "expert")
    weights = (
        P("section", both, None),
        P("section", both, None),
        P("section", both, None),
        P("section", both),
        P("section", both),
        P("section", "expert", "fsdp", None),
        P("section", "expert", "fsdp", None),
    )
    return jax.shard_map(
        shards,
        mesh=mesh,
        in_specs=(
            P(None, both, None),
            P(None, both, None),
            P(None, "fsdp"),
            P("section", None, both, None),
        )
        + weights,
        out_specs=(P("section", None, both, None), P("section", None, both, None)) + weights,
        check_vma=False,
    )
```

```python
import functools

import jax
import jax.numpy as jnp
from jax import lax
from jax.experimental import pallas as pl
from jax.experimental.pallas import tpu as pltpu
from jax.sharding import PartitionSpec as P

QUERY_HEADS = 24
KEY_VALUE_HEADS = 8
HEAD_SIZE = 64
FF = 512
NCONT = 8
EPS = 1e-06
THETA = 10000.0
LANES = 128
LOW = 64

F32 = jnp.float32
BF16 = jnp.bfloat16
ACROSS = (((1,), (1,)), ((), ()))
MESH = pl.DeviceIdType.MESH


def lasting(micros):
    return pl.CostEstimate(
        flops=int(micros * 1.1e9), bytes_accessed=int(micros * 3.6e6), transcendentals=0
    )


PAIR = 2 * HEAD_SIZE
GROUP = QUERY_HEADS // KEY_VALUE_HEADS
FACTOR = HEAD_SIZE ** (-0.5)


def swap(block, axis, bit):
    return lax.ppermute(block, axis, [(i, i ^ bit) for i in range(lax.axis_size(axis))])


def onward(block, axis):
    n = lax.axis_size(axis)
    return lax.ppermute(block, axis, [(i, (i + 1) % n) for i in range(n)])


def bits_of(axis):
    bits, bit = [], lax.axis_size(axis) // 2
    while bit:
        bits.append(bit)
        bit //= 2
    return bits


def pick(block, index, axis=0):
    return lax.dynamic_index_in_dim(block, index, axis, keepdims=False)


def after(block, *others):
    return lax.optimization_barrier((block, *others))[0]


def head(block, index):
    return block[..., index * HEAD_SIZE : (index + 1) * HEAD_SIZE]


def tie(block, *others):
    def body(*refs):
        pass

    return pl.pallas_call(
        body,
        out_shape=jax.ShapeDtypeStruct(block.shape, block.dtype),
        in_specs=[pl.BlockSpec(memory_space=pl.ANY)] * (1 + len(others)),
        out_specs=pl.BlockSpec(memory_space=pl.ANY),
        input_output_aliases={0: 0},
        cost_estimate=lasting(0.004),
    )(block, *others)


def peers():
    n = lax.axis_size("expert")
    me, fsdp, section = lax.axis_index("expert"), lax.axis_index("fsdp"), lax.axis_index("section")
    return (
        [{"expert": lax.rem(me + step, n)} for step in range(1, n)]
        + [{"fsdp": fsdp ^ bit} for bit in bits_of("fsdp")[:-1]]
        + [{"section": 1 - section}]
    )


def meet():
    barrier = pltpu.get_barrier_semaphore()
    others = peers()
    for other in others:
        pl.semaphore_signal(barrier, inc=1, device_id=other, device_id_type=MESH)
    pl.semaphore_wait(barrier, len(others))


class Rides:
    def __init__(self, rides):
        self.rides = rides
        self.count = len(rides)
        self.blocks = [b for b, _, _ in rides]
        self.specs = [pl.BlockSpec(memory_space=pltpu.HBM)] * self.count
        self.shapes = [jax.ShapeDtypeStruct(b.shape, b.dtype) for b in self.blocks]
        self.scratch = [pltpu.SemaphoreType.DMA((2, self.count))] if rides else []

    def copies(self, refs, outs, sems):
        n = lax.axis_size("expert")
        me, fsdp, section = lax.axis_index("expert"), lax.axis_index("fsdp"), lax.axis_index("section")
        made = []
        for k, (_, axis, where) in enumerate(self.rides):
            target = {
                "expert": lambda: lax.rem(me + where, n),
                "fsdp": lambda: fsdp ^ where,
                "section": lambda: 1 - section,
            }[axis]()
            copy = pltpu.make_async_remote_copy(
                src_ref=refs[k], dst_ref=outs[k], send_sem=sems.at[0, k], recv_sem=sems.at[1, k],
                device_id={axis: target}, device_id_type=MESH,
            )
            sends = receives = None
            if axis == "section" and where is not None:
                sends, receives = section != where, section == where
            made.append((copy, sends, receives))
        return made

    @staticmethod
    def when(condition, act):
        if condition is None:
            act()
        else:
            pl.when(condition)(act)

    def start(self, refs, outs, sems):
        for copy, sends, _ in self.copies(refs, outs, sems):
            self.when(sends, copy.start)

    def finish(self, refs, outs, sems):
        for copy, sends, receives in self.copies(refs, outs, sems):
            self.when(sends, copy.wait_send)
            self.when(receives, copy.wait_recv)


def dense_pieces(block, y_first, wait=None):
    n = lax.axis_size("expert")
    bits = bits_of("fsdp")
    early, late = (bits[:-1], bits[-1:]) if y_first else ([], bits)
    held = [(0, block)]
    for bit in early:
        held += [(mask ^ bit, swap(b, "fsdp", bit)) for mask, b in held]
    pieces = [(mask, 0, b) for mask, b in held]
    moving = held
    for step in range(1, n):
        moving = [(mask, onward(b, "expert")) for mask, b in moving]
        pieces += [(mask, step, b) for mask, b in moving]
    if wait is not None:
        mask, step, b = pieces[-1]
        pieces[-1] = (mask, step, tie(b, wait))
    for bit in late:
        pieces += [(mask ^ bit, step, swap(b, "fsdp", bit)) for mask, step, b in pieces]
    rows, columns = block.shape
    if rows % 16 == 0:
        return pieces
    whole = jnp.zeros((lax.axis_size("fsdp") * n * rows, columns), block.dtype)
    fsdp, expert = lax.axis_index("fsdp"), lax.axis_index("expert")
    for mask, step, b in pieces:
        start = ((fsdp ^ mask) * n + lax.rem(expert - step + n, n)) * rows
        whole = lax.dynamic_update_slice_in_dim(whole, b, start, 0)
    return [(0, 0, whole)]


class Pieces:
    def __init__(self, pieces):
        self.spots = [(mask, step) for mask, step, _ in pieces]
        self.blocks = [b for _, _, b in pieces]
        self.rows, self.columns = self.blocks[0].shape
        self.count = len(self.blocks)

    def copies(self, refs, whole, sems):
        n = lax.axis_size("expert")
        fsdp, expert = lax.axis_index("fsdp"), lax.axis_index("expert")
        out = []
        for k, (mask, step) in enumerate(self.spots):
            if self.count == 1:
                out.append(pltpu.make_async_copy(refs[k], whole, sems.at[k]))
                continue
            start = ((fsdp ^ mask) * n + lax.rem(expert - step + n, n)) * self.rows
            rows = pl.ds(pl.multiple_of(start, self.rows), self.rows)
            out.append(pltpu.make_async_copy(refs[k], whole.at[rows, :], sems.at[k]))
        return out


def vmem_call(body, out_shape, operands, anywhere, scratch_shapes=(), any_out=0, flops=0):
    vmem = pl.BlockSpec(memory_space=pltpu.VMEM)
    hbm = pl.BlockSpec(memory_space=pl.ANY)
    size = sum(o.size * o.dtype.itemsize for o in operands)
    return pl.pallas_call(
        body,
        out_shape=out_shape,
        in_specs=[vmem] * (len(operands) - anywhere) + [hbm] * anywhere,
        out_specs=[vmem] * (len(out_shape) - any_out) + [hbm] * any_out,
        scratch_shapes=list(scratch_shapes),
        compiler_params=pltpu.CompilerParams(vmem_limit_bytes=44 * 2**20),
        cost_estimate=lasting(0.1),
    )(*operands)


def turned(block, cosine, sine):
    half = HEAD_SIZE // 2
    wide = block.shape[1]
    lane = lax.broadcasted_iota(jnp.int32, block.shape, 1)
    partner = jnp.where(
        lane % HEAD_SIZE < half, pltpu.roll(block, wide - half, 1), pltpu.roll(block, half, 1)
    )
    return block * cosine + partner * sine


def gather_body(qkv_ref, out_ref, cot_ref, *refs):
    refs = refs[-8:]
    whole_qkv, whole_out, cots, y_sems, z_sems, cot_sems, x_sems, core_sems = refs
    n = lax.axis_size("expert")
    me, fsdp, section = lax.axis_index("expert"), lax.axis_index("fsdp"), lax.axis_index("section")
    right = lax.rem(me + 1, n)
    rows = qkv_ref.shape[0]
    half = rows // 2
    bits = bits_of("fsdp")[:-1]
    wholes = (whole_qkv, whole_out)
    core = fsdp + 1 - 2 * lax.rem(fsdp, 2)
    barrier = pltpu.get_barrier_semaphore()
    others = peers() + [{"fsdp": core}]
    for other in others:
        pl.semaphore_signal(barrier, inc=1, device_id=other, device_id_type=MESH)

    def place_of(column, step, part=None):
        start = (column * n + lax.rem(me - step + n, n)) * rows
        if part is None:
            return pl.ds(pl.multiple_of(start, 32), rows)
        return pl.ds(pl.multiple_of(start + part * half, 16), half)

    def send(w, spot, sems, index, device):
        return pltpu.make_async_remote_copy(
            src_ref=wholes[w].at[spot, :], dst_ref=wholes[w].at[spot, :],
            send_sem=sems.at[(0,) + index], recv_sem=sems.at[(1,) + index],
            device_id=device, device_id_type=MESH,
        )

    columns = [fsdp, fsdp ^ bits[0]]
    whole_qkv[place_of(fsdp, 0), :] = qkv_ref[...]
    whole_out[place_of(fsdp, 0), :] = out_ref[...]
    cots[0] = cot_ref[...]
    pl.semaphore_wait(barrier, len(others))

    def over_y(w):
        return send(w, place_of(fsdp, 0, section), y_sems, (w,), {"fsdp": columns[1]})

    def over_z(t, c, w):
        return send(w, place_of(columns[c], t, section), z_sems, (t, c, w), {"expert": right})

    def over_x(t, c, w):
        return send(w, place_of(columns[c], t, section), x_sems, (t, c, w), {"section": 1 - section})

    def over_core(t, c, w):
        return send(w, place_of(columns[c], t), core_sems, (t, c, w), {"fsdp": core})

    def cot_hop(t):
        return pltpu.make_async_remote_copy(
            src_ref=cots.at[t], dst_ref=cots.at[t + 1], send_sem=cot_sems.at[0, t],
            recv_sem=cot_sems.at[1, t], device_id={"expert": right}, device_id_type=MESH,
        )

    both = [(c, w) for c in range(2) for w in range(2)]
    for w in range(2):
        over_y(w).start()
        over_z(0, 0, w).start()
        over_core(0, 0, w).start()
    cot_hop(0).start()
    for w in range(2):
        over_y(w).wait_recv()
        over_z(0, 1, w).start()
        over_x(0, 1, w).start()
    for t in range(1, n):
        for c, w in both:
            over_z(t - 1, c, w).wait_recv()
            if t < n - 1:
                over_z(t, c, w).start()
            over_x(t, c, w).start()
        cot_hop(t - 1).wait_recv()
        if t < n - 1:
            cot_hop(t).start()
        for c, w in both:
            if t > 1 or c == 1:
                over_x(t - 1, c, w).wait_recv()
                over_core(t - 1, c, w).start()
    for c, w in both:
        over_x(n - 1, c, w).wait_recv()
        over_core(n - 1, c, w).start()
    for t in range(n):
        for c, w in both:
            over_core(t, c, w).wait_recv()
    for w in range(2):
        over_y(w).wait_send()
    for t in range(n):
        for c, w in both:
            over_core(t, c, w).wait_send()
            if t < n - 1:
                over_z(t, c, w).wait_send()
            if t > 0 or c == 1:
                over_x(t, c, w).wait_send()
    for t in range(n - 1):
        cot_hop(t).wait_send()


def gather_next(qkv, out, cot, wait):
    n, fsdp = lax.axis_size("expert"), lax.axis_size("fsdp")
    rows = qkv.shape[0]
    vmem, hbm = pl.BlockSpec(memory_space=pltpu.VMEM), pl.BlockSpec(memory_space=pl.ANY)
    dma = pltpu.SemaphoreType.DMA
    struct = jax.ShapeDtypeStruct
    return pl.pallas_call(
        gather_body,
        in_specs=[vmem] * 3 + [hbm],
        out_specs=[vmem] * 3,
        out_shape=[
            struct((n * fsdp * rows, qkv.shape[1]), BF16),
            struct((n * fsdp * rows, out.shape[1]), BF16),
            struct((n,) + cot.shape, BF16),
        ],
        scratch_shapes=[
            dma((2, 2)), dma((2, n - 1, 2, 2)), dma((2, n - 1)), dma((2, n, 2, 2)), dma((2, n, 2, 2)),
        ],
        compiler_params=pltpu.CompilerParams(
            vmem_limit_bytes=44 * 2**20, has_side_effects=True, collective_id=11
        ),
        cost_estimate=lasting(2),
    )(qkv, out, cot, wait)


def attend_pair(queries, keys, values, bias):
    lse, outs = [], []
    for pair in range(2):
        own_keys, own_values = head(keys, pair), head(values, pair)
        values_t = own_values.astype(F32).T.astype(BF16)
        for g in range(GROUP):
            own_queries = head(queries, pair * GROUP + g) * FACTOR
            scores = lax.dot_general(own_keys, own_queries, ACROSS, preferred_element_type=F32) + bias
            top = jnp.max(scores, 0, keepdims=True)
            weights = jnp.exp(scores - top)
            total = jnp.sum(weights, 0, keepdims=True)
            probs = (weights * (1.0 / total)).astype(BF16)
            outs.append(jnp.dot(values_t, probs, preferred_element_type=F32))
            lse.append(top + jnp.log(total))
    lse.append(jnp.zeros((8 - len(lse), lse[0].shape[1]), F32))
    return jnp.concatenate(outs, 0).T.astype(BF16), jnp.concatenate(lse, 0)


def attention_body(pieces, n_total, x_ref, cos_ref, sin_ref, bias_ref, *refs):
    weights, refs = refs[: pieces.count], refs[pieces.count :]
    normed_ref, q_ref, kv_ref, small_ref, attended_ref, lse_ref, out_ref = refs[:7]
    whole, sems, out_sem, send_sems, recv_sems = refs[7:]
    n = lax.axis_size("expert")
    me = lax.axis_index("expert")
    rows = x_ref.shape[0]
    pairs = kv_ref.shape[0]

    barrier = pltpu.get_barrier_semaphore()

    @pl.when(me > 0)
    def _():
        pl.semaphore_signal(barrier, inc=1, device_id={"expert": me - 1}, device_id_type=MESH)

    copies = pieces.copies(weights, whole, sems)
    for copy in copies:
        copy.start()
    x = x_ref[...].astype(F32)
    scaled = x * lax.rsqrt(jnp.mean(x * x, -1, keepdims=True) + EPS)
    for copy in copies:
        copy.wait()
    back = pltpu.make_async_copy(whole, out_ref, out_sem)
    back.start()
    columns = pieces.columns - LANES
    small = whole[:, columns:].astype(F32).T
    small_ref[...] = small
    normed = (scaled * small[n_total : n_total + 1, :]).astype(BF16)
    normed_ref[...] = normed
    block = KEY_VALUE_HEADS * HEAD_SIZE
    repeat = block // cos_ref.shape[1]
    cosine = jnp.concatenate([cos_ref[...]] * repeat, 1)
    sine = jnp.concatenate([sin_ref[...]] * repeat, 1)
    count = columns // block

    def columns_of(k):
        return jnp.dot(normed, whole[:, k * block : (k + 1) * block], preferred_element_type=F32)

    keys = turned(columns_of(count - 2), cosine, sine).astype(BF16)
    values = columns_of(count - 1).astype(BF16)
    for p in range(pairs):
        kv_ref[p, 0, 0] = keys[:, p * PAIR : (p + 1) * PAIR]
        kv_ref[p, 0, 1] = values[:, p * PAIR : (p + 1) * PAIR]

        for t in range(1, n):

            @pl.when(me < t)
            def _():
                kv_ref[p, t] = jnp.zeros(kv_ref.shape[2:], BF16)

    def hop(p, t):
        return pltpu.make_async_remote_copy(
            src_ref=kv_ref.at[p, t], dst_ref=kv_ref.at[p, t + 1], send_sem=send_sems.at[p, t],
            recv_sem=recv_sems.at[p, t], device_id={"expert": me + 1}, device_id_type=MESH,
        )

    def forward_step(p, t):
        if t > 0:

            @pl.when(me >= t)
            def _():
                hop(p, t - 1).wait_recv()

        if t < n - 1:

            @pl.when((me < n - 1) & (me >= t))
            def _():
                hop(p, t).start()

    @pl.when(me < n - 1)
    def _():
        pl.semaphore_wait(barrier, 1)

    for p in range(pairs):
        forward_step(p, 0)
    for k in range(count - 2):
        q_ref[:, k * block : (k + 1) * block] = turned(columns_of(k), cosine, sine).astype(BF16)
    for t in range(1, n - 1):
        for p in range(pairs):
            forward_step(p, t)
    wide = 2 * GROUP * HEAD_SIZE

    def one(p, carry):
        forward_step(p, n - 1)
        spot = pl.ds(pl.multiple_of(p * wide, LANES), wide)
        pair = kv_ref[p]
        attended, lse = attend_pair(
            q_ref[:, spot], pair[:, 0].reshape(n * rows, PAIR), pair[:, 1].reshape(n * rows, PAIR),
            bias_ref[...],
        )
        attended_ref[:, spot] = attended
        lse_ref[p] = lse
        return carry

    lax.fori_loop(0, pairs, one, 0)
    for t in range(n - 1):

        @pl.when((me < n - 1) & (me >= t))
        def _():
            for p in range(pairs):
                hop(p, t).wait_send()

    back.wait()


def attention_forward(x, layout, pieces, n_total, identity):
    bias, tables, _ = layout
    n = lax.axis_size("expert")
    rows, width = x.shape
    columns = pieces.columns
    pairs = KEY_VALUE_HEADS // 2
    vmem, hbm = pl.BlockSpec(memory_space=pltpu.VMEM), pl.BlockSpec(memory_space=pl.ANY)
    struct = jax.ShapeDtypeStruct
    dma = pltpu.SemaphoreType.DMA
    heads = QUERY_HEADS * HEAD_SIZE
    return pl.pallas_call(
        functools.partial(attention_body, pieces, n_total),
        in_specs=[vmem] * 4 + [hbm] * pieces.count,
        out_specs=[vmem] * 6 + [hbm],
        out_shape=[
            struct((rows, width), BF16),
            struct((rows, heads), BF16),
            struct((pairs, n, 2, rows, PAIR), BF16),
            struct((LANES, width), F32),
            struct((rows, heads), BF16),
            struct((pairs, 8, rows), F32),
            struct((width, columns), BF16),
        ],
        scratch_shapes=[
            pltpu.VMEM((width, columns), BF16), dma((pieces.count,)), dma,
            dma((pairs, n - 1)), dma((pairs, n - 1)),
        ],
        compiler_params=pltpu.CompilerParams(
            vmem_limit_bytes=48 * 2**20, has_side_effects=True, collective_id=identity
        ),
        cost_estimate=lasting(0.64),
    )(x, *tables, bias, *pieces.blocks)


def route_body(pieces, n_total, x_ref, attended_ref, small_ref, route_ref, *refs):
    weights, refs = refs[: pieces.count], refs[pieces.count :]
    hidden_ref, ext_ref, out_ref, whole, sems, out_sem = refs
    copies = pieces.copies(weights, whole, sems)
    for copy in copies:
        copy.start()
    for copy in copies:
        copy.wait()
    back = pltpu.make_async_copy(whole, out_ref, out_sem)
    back.start()
    rows, width = x_ref.shape
    block = 512
    for k in range(0, width, block):
        hidden_ref[:, k : k + block] = x_ref[:, k : k + block].astype(F32) + jnp.dot(
            attended_ref[...], whole[:, k : k + block], preferred_element_type=F32
        )
    hidden = hidden_ref[...]
    scale = lax.rsqrt(jnp.mean(hidden * hidden, -1, keepdims=True) + EPS)
    normed = (hidden * scale * small_ref[n_total + 1 : n_total + 2, :]).astype(BF16)
    ext_ref[:, :width] = normed
    logits = lax.dot_general(
        normed, small_ref[...].astype(BF16), ACROSS, preferred_element_type=F32
    )
    lane = lax.broadcasted_iota(jnp.int32, logits.shape, 1)
    chosen = lane == route_ref[:, 0:1]
    for k in range(1, route_ref.shape[1]):
        chosen = chosen | (lane == route_ref[:, k : k + 1])
    logits = jnp.where(chosen, logits, -1e30)
    weights = jnp.where(chosen, jnp.exp(logits - jnp.max(logits, 1, keepdims=True)), 0.0)
    gates = weights / jnp.sum(weights, 1, keepdims=True)
    high = gates.astype(BF16).astype(F32)
    ext_ref[:, width:] = (high + pltpu.roll(gates - high, LOW, 1)).astype(BF16)
    back.wait()


def route_tokens(x, attended, small, route, pieces, n_total):
    rows, width = x.shape
    return vmem_call(
        functools.partial(route_body, pieces, n_total),
        [
            jax.ShapeDtypeStruct((rows, width), F32),
            jax.ShapeDtypeStruct((rows, width + LANES), BF16),
            jax.ShapeDtypeStruct((width, pieces.columns), BF16),
        ],
        [x, attended, small, route, *pieces.blocks],
        pieces.count,
        [
            pltpu.VMEM((width, pieces.columns), BF16),
            pltpu.SemaphoreType.DMA((pieces.count,)),
            pltpu.SemaphoreType.DMA,
        ],
        1,
        2 * rows * width * pieces.columns,
    )


def joined(lanes):
    lane = lax.broadcasted_iota(jnp.int32, lanes.shape, 1)
    return jnp.where(lane < LOW, lanes + pltpu.roll(lanes, LOW, 1), 0.0)


def route_back_body(
    n_total, summed_ref, hidden_ref, lanes_ref, grad_ref, small_ref, weight_ref,
    grad_hidden_ref, grad_attn_ref, grad_attended_ref, grad_logits_ref, gain_ref,
):
    rows, width = hidden_ref.shape
    gates = joined(lanes_ref[:, width:].astype(F32))
    grad_gates = joined(summed_ref[:, width:])
    grad_logits = gates * (grad_gates - jnp.sum(gates * grad_gates, 1, keepdims=True))
    grad_logits = grad_logits.astype(BF16)
    grad_logits_ref[...] = grad_logits
    grad_normed = (
        summed_ref[:, :width]
        + jnp.dot(grad_logits, small_ref[...].astype(BF16), preferred_element_type=F32)
    )
    hidden = hidden_ref[...]
    scale = lax.rsqrt(jnp.mean(hidden * hidden, -1, keepdims=True) + EPS)
    unit = hidden * scale
    gain = jnp.sum(grad_normed * unit, 0, keepdims=True)
    gain_ref[...] = jnp.broadcast_to(gain, gain_ref.shape)
    lifted = grad_normed * small_ref[n_total + 1 : n_total + 2, :]
    grad_hidden = (
        grad_ref[...].astype(F32)
        + scale * lifted
        - unit * (scale * jnp.mean(lifted * unit, -1, keepdims=True))
    )
    grad_hidden_ref[...] = grad_hidden
    grad_attn = grad_hidden.astype(BF16)
    grad_attn_ref[...] = grad_attn
    block = 512
    for k in range(0, width, block):
        grad_attended_ref[:, k : k + block] = lax.dot_general(
            grad_attn, weight_ref[k : k + block, :], ACROSS, preferred_element_type=F32
        ).astype(BF16)


def route_back(summed, hidden, x_ext, grad, small, weight, n_total):
    rows, width = hidden.shape
    return vmem_call(
        functools.partial(route_back_body, n_total),
        [
            jax.ShapeDtypeStruct((rows, width), F32),
            jax.ShapeDtypeStruct((rows, width), BF16),
            jax.ShapeDtypeStruct((rows, weight.shape[0]), BF16),
            jax.ShapeDtypeStruct((rows, LANES), BF16),
            jax.ShapeDtypeStruct((8, width), F32),
        ],
        [summed, hidden, x_ext, grad, small, weight],
        0,
        flops=2 * rows * width * width,
    )


def project_back_body(
    n_total, columns, grad_q_ref, grad_kv_ref, cos_ref, sin_ref, x_ref, grad_hidden_ref, small_ref,
    weight_ref, grad_mixed_ref, grad_x_ref, gain_ref,
):
    rows, width = x_ref.shape
    block = KEY_VALUE_HEADS * HEAD_SIZE
    repeat = block // cos_ref.shape[1]
    cosine = jnp.concatenate([cos_ref[...]] * repeat, 1)
    sine = jnp.concatenate([sin_ref[...]] * repeat, 1)
    pairs = grad_kv_ref.shape[0]
    grad_keys = jnp.concatenate([grad_kv_ref[p, 0] for p in range(pairs)], 1)
    grad_values = jnp.concatenate([grad_kv_ref[p, 1] for p in range(pairs)], 1)
    query_columns = columns - 2 * block
    grad_mixed_ref[:, :query_columns] = grad_q_ref[...]
    grad_mixed_ref[:, query_columns : query_columns + block] = turned(grad_keys, cosine, -sine).astype(BF16)
    grad_mixed_ref[:, query_columns + block :] = grad_values.astype(BF16)
    grad_mixed = grad_mixed_ref[...]
    parts = []
    step = 512
    for k in range(0, width, step):
        parts.append(
            lax.dot_general(
                grad_mixed, weight_ref[k : k + step, :columns], ACROSS, preferred_element_type=F32
            )
        )
    grad_normed = jnp.concatenate(parts, 1)
    x = x_ref[...].astype(F32)
    scale = lax.rsqrt(jnp.mean(x * x, -1, keepdims=True) + EPS)
    unit = x * scale
    gain = jnp.sum(grad_normed * unit, 0, keepdims=True)
    gain_ref[...] = jnp.broadcast_to(gain, gain_ref.shape)
    lifted = grad_normed * small_ref[n_total : n_total + 1, :]
    grad_x_ref[...] = (
        grad_hidden_ref[...]
        + scale * lifted
        - unit * (scale * jnp.mean(lifted * unit, -1, keepdims=True))
    ).astype(BF16)


def project_back(grad_q, grad_kv, tables, x, grad_hidden, small, weight, n_total):
    rows, width = x.shape
    columns = weight.shape[1] - LANES
    return vmem_call(
        functools.partial(project_back_body, n_total, columns),
        [
            jax.ShapeDtypeStruct((rows, columns), BF16),
            jax.ShapeDtypeStruct((rows, width), BF16),
            jax.ShapeDtypeStruct((8, width), F32),
        ],
        [grad_q, grad_kv, *tables, x, grad_hidden, small, weight],
        0,
        flops=2 * rows * width * columns,
    )


def product_body(
    extra, left_ref, right_ref, normed_ref, logits_ref, gain_one_ref, gain_two_ref, left_two_ref, right_two_ref,
    out_ref, blocks, send_sems, recv_sems,
):
    highs, rows = out_ref.shape[0], out_ref.shape[1]
    columns = right_ref.shape[1]
    fsdp = lax.axis_index("fsdp")
    core = fsdp % 2
    other = fsdp + 1 - 2 * core
    barrier = pltpu.get_barrier_semaphore()
    pl.semaphore_signal(barrier, inc=1, device_id={"fsdp": other}, device_id_type=MESH)

    def send(high):
        return pltpu.make_async_remote_copy(
            src_ref=blocks.at[0, high], dst_ref=blocks.at[1, high], send_sem=send_sems.at[high],
            recv_sem=recv_sems.at[high], device_id={"fsdp": other}, device_id_type=MESH,
        )

    def products(high, whose):
        spot = pl.ds(pl.multiple_of((high * 2 + whose) * rows, LANES), rows)

        def turned_rows(ref):
            return ref[:, spot].astype(F32).T.astype(BF16)

        step = 512
        left = turned_rows(left_ref)
        for k in range(0, columns, step):
            yield k, step, jnp.dot(left, right_ref[:, k : k + step], preferred_element_type=F32)
        small = jnp.dot(turned_rows(normed_ref), logits_ref[...], preferred_element_type=F32)
        lane = lax.broadcasted_iota(jnp.int32, small.shape, 1)
        one = gain_one_ref[:, spot].T[:, 0:1]
        two = gain_two_ref[:, spot].T[:, 0:1]
        yield columns, LANES, jnp.where(lane == extra, one, jnp.where(lane == extra + 1, two, small))
        left = turned_rows(left_two_ref)
        for k in range(0, right_two_ref.shape[1], step):
            yield columns + LANES + k, step, jnp.dot(
                left, right_two_ref[:, k : k + step], preferred_element_type=F32
            )

    for high in range(highs):
        for start, size, value in products(high, 1 - core):
            blocks[0, high, :, start : start + size] = value.astype(BF16)
        if high == 0:
            pl.semaphore_wait(barrier, 1)
        send(high).start()
    for high in range(highs):
        send(high).wait_recv()
        for start, size, value in products(high, core):
            arrived = blocks[1, high, :, start : start + size].astype(F32)
            out_ref[high, :, start : start + size] = (value + arrived).astype(BF16)
    for high in range(highs):
        send(high).wait_send()


def dense_product(left, right, extra, small, second):
    tokens, width = left.shape
    highs = lax.axis_size("fsdp") // 2
    rows = width // (2 * highs)
    columns = right.shape[1] + LANES + second[1].shape[1]
    vmem = pl.BlockSpec(memory_space=pltpu.VMEM)
    operands = [left, right, *small, *second]
    return pl.pallas_call(
        functools.partial(product_body, extra),
        in_specs=[vmem] * len(operands),
        out_specs=vmem,
        out_shape=jax.ShapeDtypeStruct((highs, rows, columns), BF16),
        scratch_shapes=[
            pltpu.VMEM((2, highs, rows, columns), BF16),
            pltpu.SemaphoreType.DMA((highs,)),
            pltpu.SemaphoreType.DMA((highs,)),
        ],
        compiler_params=pltpu.CompilerParams(
            vmem_limit_bytes=48 * 2**20, has_side_effects=True, collective_id=6
        ),
        cost_estimate=lasting(0.3),
    )(*operands)


def experts_body(mode, section, rides, extra, *refs):
    forward, backward = mode != "backward", mode != "forward"
    refs = list(refs)
    take = lambda count: [refs.pop(0) for _ in range(count)]
    if mode == "backward":
        moving_ref, ext_ref, both_in = take(3)
        grads_ref = None
    else:
        (moving_ref,) = take(1)
        grads_ref = take(1)[0] if mode == "both" else None
    gate_up_ref, down_ref = take(2)
    riding = take(rides.count)
    take(extra)
    out_ref, ring_out = take(2)
    if mode == "forward":
        (both_out,) = take(1)
    else:
        grad_both_out, act_out = take(2)
        parts_out = take(1)[0] if mode == "both" else None
    arrived = take(rides.count)
    gate_up, down, weight_sems, ring, ring_sems, out_sems = take(6)
    sums, sum_sems, total = take(3)
    if mode == "forward":
        stage, stage_sems = take(2)
    else:
        stage, act_stage, stage_sems = take(3)
        if mode == "both":
            part_total, part_stage, part_sems = take(3)
        else:
            lanes, lane_sem, both_stage, both_sems = take(4)

    n = lax.axis_size("expert")
    me = lax.axis_index("expert")
    right, left = lax.rem(me + 1, n), lax.rem(me + n - 1, n)
    experts, fsdp = gate_up.shape[0], gate_up.shape[1]
    rows = moving_ref.shape[0]
    width = down.shape[3]

    if rides.count:
        ride_sems = refs.pop()
        meet()
        rides.start(riding, arrived, ride_sems)
    else:
        barrier = pltpu.get_barrier_semaphore()
        pl.semaphore_signal(barrier, inc=1, device_id={"expert": left}, device_id_type=MESH)

    loads = []
    for e in range(experts):
        of = pl.ds(section * fsdp, fsdp)
        loads.append(
            [
                pltpu.make_async_copy(gate_up_ref.at[of, e], gate_up.at[e], weight_sems.at[0, e]),
                pltpu.make_async_copy(down_ref.at[of, e], down.at[e], weight_sems.at[1, e]),
            ]
        )
        for load in loads[-1]:
            load.start()
    if mode == "backward":
        fetch = lambda k: pltpu.make_async_copy(
            both_in.at[k // experts, k % experts], both_stage.at[k % 2], both_sems.at[k % 2]
        )
        fetch(0).start()
        lane_copy = pltpu.make_async_copy(ext_ref.at[:, :, pl.ds(width, LANES)], lanes, lane_sem)
        lane_copy.start()
    ring[0] = moving_ref[...]
    if not rides.count:
        pl.semaphore_wait(barrier, 1)

    hops = [
        pltpu.make_async_remote_copy(
            src_ref=ring.at[t], dst_ref=ring.at[t + 1], send_sem=ring_sems.at[0, t],
            recv_sem=ring_sems.at[1, t], device_id={"expert": right}, device_id_type=MESH,
        )
        for t in range(n - 1)
    ]
    carries = [
        pltpu.make_async_remote_copy(
            src_ref=sums.at[0, t], dst_ref=sums.at[1, t], send_sem=sum_sems.at[0, t],
            recv_sem=sum_sems.at[1, t], device_id={"expert": right}, device_id_type=MESH,
        )
        for t in range(n - 1)
    ]
    stores = [pltpu.make_async_copy(ring.at[t], ring_out.at[t], out_sems.at[t]) for t in range(n)]
    if mode == "backward":
        lane_copy.wait()

    for t in range(n):
        if t > 0:
            hops[t - 1].wait_recv()
        if t < n - 1:
            hops[t].start()
        stores[t].start()
        total[...] = jnp.zeros_like(total)
        if mode == "both":
            part_total[...] = jnp.zeros_like(part_total)

        def one(e, carry):
            k = t * experts + e
            slot = lax.rem(k, 2)
            which = me * experts + e
            weights_one = gate_up[e].reshape(fsdp * gate_up.shape[2], gate_up.shape[3])
            weights_two = down[e].reshape(fsdp * down.shape[2], width)
            if mode == "backward":
                weight = gate_of(lanes[t], which)
                fetch(k).wait()

                @pl.when(k + 1 < n * experts)
                def _():
                    pltpu.make_async_copy(
                        both_in.at[lax.div(k + 1, experts), lax.rem(k + 1, experts)],
                        both_stage.at[1 - slot], both_sems.at[1 - slot],
                    ).start()

                gate = both_stage[slot, :, :FF].astype(F32)
                up = both_stage[slot, :, FF:].astype(F32)
            else:
                weight = gate_of(ring[t, :, width:], which)
                both = jnp.dot(ring[t, :, :width], weights_one, preferred_element_type=F32)
                gate, up = both[:, :FF], both[:, FF:]
            sigma = jax.nn.sigmoid(gate)
            silu = gate * sigma
            act = silu * up
            gated = (act * weight).astype(BF16)
            if forward:
                part = jnp.dot(gated, weights_two, preferred_element_type=F32)
                if mode == "forward":
                    total[...] += part
                else:
                    part_total[...] += part

            if mode == "forward":

                @pl.when(k >= 2)
                def _():
                    pltpu.make_async_copy(stage.at[slot], both_out.at[t, e], stage_sems.at[slot]).wait()

                stage[slot] = both.astype(BF16)
                pltpu.make_async_copy(stage.at[slot], both_out.at[t, e], stage_sems.at[slot]).start()
            else:
                grad_rows = ring[t] if mode == "backward" else grads_ref[t]
                grad = lax.dot_general(grad_rows, weights_two, ACROSS, preferred_element_type=F32)
                grad_weight = jnp.sum(grad * act, 1, keepdims=True)
                grad_act = grad * weight
                grad_gate = grad_act * up * (sigma * (1.0 + gate * (1.0 - sigma)))
                grad_both = jnp.concatenate([grad_gate, grad_act * silu], 1).astype(BF16)
                total[:, :width] += lax.dot_general(
                    grad_both, weights_one, ACROSS, preferred_element_type=F32
                )
                high = grad_weight.astype(BF16).astype(F32)
                lane = lax.broadcasted_iota(jnp.int32, (rows, LANES), 1)
                total[:, width:] += jnp.where(
                    lane == which, high, jnp.where(lane == which + LOW, grad_weight - high, 0.0)
                )

                @pl.when(k >= 2)
                def _():
                    pltpu.make_async_copy(
                        stage.at[slot], grad_both_out.at[t, e], stage_sems.at[0, slot]
                    ).wait()
                    pltpu.make_async_copy(
                        act_stage.at[slot], act_out.at[t, e], stage_sems.at[1, slot]
                    ).wait()

                stage[slot] = grad_both
                act_stage[slot] = gated
                pltpu.make_async_copy(stage.at[slot], grad_both_out.at[t, e], stage_sems.at[0, slot]).start()
                pltpu.make_async_copy(act_stage.at[slot], act_out.at[t, e], stage_sems.at[1, slot]).start()
            return carry

        if t == 0:
            for e in range(experts):
                for load in loads[e]:
                    load.wait()
                one(e, 0)
        else:
            lax.fori_loop(0, experts, one, 0)

        if mode == "both":
            if t >= 2:
                pltpu.make_async_copy(part_stage.at[t % 2], parts_out.at[t - 2], part_sems.at[t % 2]).wait()
            part_stage[t % 2] = part_total[...].astype(BF16)
            pltpu.make_async_copy(part_stage.at[t % 2], parts_out.at[t], part_sems.at[t % 2]).start()
        if t == 0:
            out_ref[...] = total[...]
        else:
            if t > 1:
                carries[t - 2].wait_recv()
                sums[0, t - 1] = (total[...] + sums[1, t - 2].astype(F32)).astype(BF16)
            else:
                sums[0, 0] = total[...].astype(BF16)
            carries[t - 1].start()

    carries[n - 2].wait_recv()
    out_ref[...] += sums[1, n - 2].astype(F32)
    for t in range(n - 1):
        hops[t].wait_send()
        carries[t].wait_send()
    for store in stores:
        store.wait()
    last = n * experts - 1
    for k in (last - 1, last):
        t, e, slot = k // experts, k % experts, k % 2
        if mode == "forward":
            pltpu.make_async_copy(stage.at[slot], both_out.at[t, e], stage_sems.at[slot]).wait()
        else:
            pltpu.make_async_copy(stage.at[slot], grad_both_out.at[t, e], stage_sems.at[0, slot]).wait()
            pltpu.make_async_copy(act_stage.at[slot], act_out.at[t, e], stage_sems.at[1, slot]).wait()
    if mode == "both":
        for t in (n - 2, n - 1):
            pltpu.make_async_copy(part_stage.at[t % 2], parts_out.at[t], part_sems.at[t % 2]).wait()


def gate_of(lanes, which):
    place_of = lax.broadcasted_iota(jnp.int32, lanes.shape, 1)
    chosen = (place_of == which) | (place_of == which + LOW)
    return jnp.sum(jnp.where(chosen, lanes.astype(F32), 0.0), 1, keepdims=True)


def run_experts(mode, section, moving, inputs, gate_up, down, others=(), rides=()):
    rides = Rides(rides)
    n = lax.axis_size("expert")
    fsdp, experts = gate_up.shape[0] // 2, gate_up.shape[1]
    columns, width = gate_up.shape[3], down.shape[3]
    rows = moving.shape[0]
    wide = width + LANES
    vmem, hbm = pl.BlockSpec(memory_space=pltpu.VMEM), pl.BlockSpec(memory_space=pl.ANY)
    struct = jax.ShapeDtypeStruct
    dma = pltpu.SemaphoreType.DMA
    sum_wide = width if mode == "forward" else wide
    out_shape = [struct((rows, sum_wide), F32), struct((n,) + moving.shape, BF16)]
    scratch = [
        pltpu.VMEM((experts, fsdp) + gate_up.shape[2:], BF16),
        pltpu.VMEM((experts, fsdp) + down.shape[2:], BF16),
        dma((2, experts)),
        pltpu.VMEM((n,) + moving.shape, BF16),
        dma((2, n - 1)),
        dma((n,)),
        pltpu.VMEM((2, n - 1, rows, sum_wide), BF16),
        dma((2, n - 1)),
        pltpu.VMEM((rows, sum_wide), F32),
    ]
    if mode == "forward":
        out_shape += [struct((n, experts, rows, columns), BF16)]
        scratch += [pltpu.VMEM((2, rows, columns), BF16), dma((2,))]
    else:
        out_shape += [struct((n, experts, rows, columns), BF16), struct((n, experts, rows, FF), BF16)]
        scratch += [pltpu.VMEM((2, rows, columns), BF16), pltpu.VMEM((2, rows, FF), BF16), dma((2, 2))]
        if mode == "both":
            out_shape += [struct((n, rows, width), BF16)]
            scratch += [pltpu.VMEM((rows, width), F32), pltpu.VMEM((2, rows, width), BF16), dma((2,))]
        else:
            scratch += [
                pltpu.VMEM((n, rows, LANES), BF16), dma, pltpu.VMEM((2, rows, columns), BF16), dma((2,)),
            ]
    in_spec = {"forward": [vmem], "both": [vmem, vmem], "backward": [vmem, hbm, hbm]}[mode]
    products = {"forward": 1, "both": 2, "backward": 1}[mode]
    return pl.pallas_call(
        functools.partial(experts_body, mode, section, rides, len(others)),
        in_specs=in_spec + [hbm] * 2 + rides.specs + [hbm] * len(others),
        out_specs=[vmem] + [hbm] * (len(out_shape) - 1) + rides.specs,
        out_shape=out_shape + rides.shapes,
        scratch_shapes=scratch + rides.scratch,
        compiler_params=pltpu.CompilerParams(
            vmem_limit_bytes=56 * 2**20,
            has_side_effects=True,
            collective_id={"forward": 1, "both": 2, "backward": 3}[mode],
        ),
        cost_estimate=lasting(2.3),
    )(moving, *inputs, gate_up, down, *rides.blocks, *others)


def query_layout(segment, token_rows):
    n = lax.axis_size("expert")
    me = lax.axis_index("expert")
    offset = me * token_rows
    labels = jnp.arange(NCONT + 1, dtype=jnp.int32)
    member = (segment[:, None] == labels[None, :]).astype(jnp.int32)
    totals = jnp.sum(member, 0)
    starts = jnp.cumsum(totals) - totals
    query_seg = lax.dynamic_slice_in_dim(segment, offset, token_rows)
    query_idx = offset + jnp.arange(token_rows, dtype=jnp.int32)
    first = jnp.sum((query_seg[:, None] == labels[None, :]).astype(jnp.int32) * starts[None, :], 1)
    query_pos = jnp.where(query_seg == 0, query_idx, totals[0] + query_idx - first)
    parts = []
    for step in range(n):
        base = lax.rem(me - step + n, n) * token_rows
        key_seg = lax.dynamic_slice_in_dim(segment, base, token_rows)
        key_idx = base + jnp.arange(token_rows, dtype=jnp.int32)
        allowed = (key_idx[:, None] <= query_idx[None, :]) & (
            (key_seg[:, None] == 0) | (key_seg[:, None] == query_seg[None, :])
        )
        parts.append(jnp.where(allowed, 0.0, -1e30).astype(F32))
    half = HEAD_SIZE // 2
    freq = THETA ** (-jnp.arange(half, dtype=F32) / half)
    angle = query_pos.astype(F32)[:, None] * freq[None, :]
    cosine, sine = jnp.cos(angle), jnp.sin(angle)
    wide = jnp.concatenate([cosine] * 4, 1), jnp.concatenate([-sine, sine, -sine, sine], 1)
    return jnp.concatenate(parts, 0), wide, (cosine.T, sine.T)


def attention_back_body(rides, q_ref, kv_ref, grad_ref, bias_ref, lse_ref, cos_ref, sin_ref, *refs):
    riding, refs = refs[: rides.count], refs[rides.count :]
    grad_q_ref, out_ref = refs[:2]
    landed, refs = refs[2 : 2 + rides.count], refs[2 + rides.count :]
    parts, sums, send_sems, recv_sems = refs[:4]
    n = lax.axis_size("expert")
    me = lax.axis_index("expert")
    pairs, _, _, rows, _ = kv_ref.shape
    half = HEAD_SIZE // 2
    wide = 2 * GROUP * HEAD_SIZE
    if rides.count:
        meet()
        rides.start(riding, landed, refs[4])
    else:
        barrier = pltpu.get_barrier_semaphore()

        @pl.when(me < n - 1)
        def _():
            pl.semaphore_signal(barrier, inc=1, device_id={"expert": me + 1}, device_id_type=MESH)

    @pl.when(me == n - 1)
    def _():
        sums[1] = jnp.zeros(sums.shape[1:], BF16)

    def send(p, step):
        return pltpu.make_async_remote_copy(
            src_ref=sums.at[0, p, step - 1], dst_ref=sums.at[1, p, step - 1],
            send_sem=send_sems.at[p, step - 1], recv_sem=recv_sems.at[p, step - 1],
            device_id={"expert": me - 1}, device_id_type=MESH,
        )

    def arrived(p, step):
        @pl.when(me < n - 1)
        def _():
            send(p, step).wait_recv()

        return sums[1, p, step - 1].astype(F32)

    def move(p, step):
        value = parts[p, n - step]
        if step > 1:
            value = value + arrived(p, step - 1)
        if step == n:
            out_ref[p] = value
        else:
            sums[0, p, step - 1] = value.astype(BF16)

            @pl.when(me > 0)
            def _():
                send(p, step).start()

    def compute(p):
        cosine, sine = cos_ref[...], sin_ref[...]
        spot = pl.ds(pl.multiple_of(p * wide, LANES), wide)
        queries_all, grads_all = q_ref[:, spot], grad_ref[:, spot]
        block = kv_ref[p]
        keys_all, values_all = block[:, 0].reshape(n * rows, PAIR), block[:, 1].reshape(n * rows, PAIR)
        grad_q = []
        for pair in range(2):
            keys, values = head(keys_all, pair), head(values_all, pair)
            keys_t = keys.astype(F32).T.astype(BF16)
            grad_keys, grad_values = None, None
            for g in range(GROUP):
                h = pair * GROUP + g
                queries = head(queries_all, h) * FACTOR
                grad = head(grads_all, h)
                scores = lax.dot_general(keys, queries, ACROSS, preferred_element_type=F32) + bias_ref[...]
                probs = jnp.exp(scores - lse_ref[p, h : h + 1, :])
                grad_probs = lax.dot_general(values, grad, ACROSS, preferred_element_type=F32)
                product = probs * grad_probs
                inner = jnp.sum(product, 0, keepdims=True)
                grad_scores = (product - probs * inner).astype(BF16)
                dv = jnp.dot(probs.astype(BF16), grad, preferred_element_type=F32)
                dk = jnp.dot(grad_scores, queries, preferred_element_type=F32)
                grad_values = dv if grad_values is None else grad_values + dv
                grad_keys = dk if grad_keys is None else grad_keys + dk
                dq = jnp.dot(keys_t, grad_scores, preferred_element_type=F32) * FACTOR
                upper, lower = dq[:half], dq[half:]
                grad_q += [upper * cosine + lower * sine, lower * cosine - upper * sine]
            lanes = slice(pair * HEAD_SIZE, (pair + 1) * HEAD_SIZE)
            for t in range(n):
                parts[p, t, 0, :, lanes] = grad_keys[t * rows : (t + 1) * rows]
                parts[p, t, 1, :, lanes] = grad_values[t * rows : (t + 1) * rows]
        grad_q_ref[:, spot] = jnp.concatenate(grad_q, 0).T.astype(BF16)

    compute(0)
    if not rides.count:

        @pl.when(me > 0)
        def _():
            pl.semaphore_wait(barrier, 1)

    move(0, 1)

    def one(p, carry):
        compute(p)
        move(p, 1)
        for step in range(2, n + 1):

            @pl.when(p >= step - 1)
            def _():
                move(p - (step - 1), step)

        return carry

    lax.fori_loop(1, pairs, one, 0)
    for late in range(pairs, pairs + n - 1):
        for step in range(2, n + 1):
            if 0 <= late - (step - 1) < pairs:
                move(late - (step - 1), step)

    @pl.when(me > 0)
    def _():
        for p in range(pairs):
            for step in range(1, n):
                send(p, step).wait_send()

    if rides.count:
        rides.finish(riding, landed, refs[4])


def attention_backward(queries, kv, grad, lse, layout, rides=(), identity=5):
    bias, _, turned_tables = layout
    rides = Rides(rides)
    pairs, n, _, rows, _ = kv.shape
    vmem = pl.BlockSpec(memory_space=pltpu.VMEM)
    dma = pltpu.SemaphoreType.DMA
    out = pl.pallas_call(
        functools.partial(attention_back_body, rides),
        in_specs=[vmem] * 7 + rides.specs,
        out_specs=[vmem] * 2 + rides.specs,
        out_shape=[
            jax.ShapeDtypeStruct(queries.shape, BF16),
            jax.ShapeDtypeStruct((pairs, 2, rows, PAIR), F32),
        ]
        + rides.shapes,
        scratch_shapes=[
            pltpu.VMEM((pairs, n, 2, rows, PAIR), F32),
            pltpu.VMEM((2, pairs, n - 1, 2, rows, PAIR), BF16),
            dma((pairs, n - 1)),
            dma((pairs, n - 1)),
        ]
        + rides.scratch,
        compiler_params=pltpu.CompilerParams(
            vmem_limit_bytes=48 * 2**20, has_side_effects=True, collective_id=identity
        ),
        cost_estimate=lasting(0.9),
    )(queries, kv, grad, bias, lse, *turned_tables, *rides.blocks)
    return out[0], out[1], out[2:]


def ring_of(block, axis="expert"):
    blocks = [block]
    for _ in range(lax.axis_size(axis) - 1):
        blocks.append(onward(blocks[-1], axis))
    return blocks


def down_body(grads_ref, acts_ref, *refs):
    out_ref, turned_act = refs[-2], refs[-1]
    n, rows, width = grads_ref.shape
    for t in range(n):
        turned_act[:, t * rows : (t + 1) * rows] = acts_ref[t, 0].astype(F32).T.astype(BF16)
    step = 512
    for k in range(0, width, step):
        out_ref[0, :, k : k + step] = jnp.dot(
            turned_act[...], grads_ref[:, :, k : k + step].reshape(n * rows, step),
            preferred_element_type=F32,
        ).astype(BF16)


def down_products(grads, acts, others=()):
    n, rows, width = grads.shape
    count = acts.shape[1]
    return pl.pallas_call(
        down_body,
        grid=(count,),
        in_specs=[
            pl.BlockSpec((n, rows, width), lambda e: (0, 0, 0)),
            pl.BlockSpec((n, 1, rows, FF), lambda e: (0, e, 0, 0)),
        ]
        + [pl.BlockSpec(memory_space=pl.ANY)] * len(others),
        out_specs=pl.BlockSpec((1, FF, width), lambda e: (e, 0, 0)),
        out_shape=jax.ShapeDtypeStruct((count, FF, width), BF16),
        scratch_shapes=[pltpu.VMEM((FF, n * rows), BF16)],
        compiler_params=pltpu.CompilerParams(vmem_limit_bytes=44 * 2**20),
        cost_estimate=lasting(0.22),
    )(grads, acts, *others)


def gate_up_body(rides, exts_ref, grads_ref, *refs):
    riding, refs = refs[: rides.count], refs[len(refs) - rides.count - 4 :]
    low_ref, high_ref, arrived, sems, turned_x = refs[0], refs[1], refs[2 : 2 + rides.count], refs[-2], refs[-1]
    e = pl.program_id(0)
    n, _, rows, columns = grads_ref.shape
    width = turned_x.shape[0]
    cut = pl.num_programs(0) - 1

    @pl.when(e == 0)
    def _():
        meet()
        rides.start(riding, arrived, sems)
        for t in range(n):
            turned_x[:, t * rows : (t + 1) * rows] = exts_ref[t, :, :width].astype(F32).T.astype(BF16)

    def fill(out_ref):
        step = 256
        for k in range(0, columns, step):
            out_ref[0, :, k : k + step] = jnp.dot(
                turned_x[...], grads_ref[:, 0, :, k : k + step].reshape(n * rows, step),
                preferred_element_type=F32,
            ).astype(BF16)

    @pl.when(e < cut)
    def _():
        fill(low_ref)

    @pl.when(e >= cut)
    def _():
        fill(high_ref)

    @pl.when(e == pl.num_programs(0) - 1)
    def _():
        rides.finish(riding, arrived, sems)


def gate_up_products(exts, grads, rides, identity, others=()):
    rides = Rides(rides)
    n, rows, wide = exts.shape
    width = wide - LANES
    count, columns = grads.shape[1], grads.shape[3]
    cut = count - 1
    hbm = pl.BlockSpec(memory_space=pl.ANY)
    out = pl.pallas_call(
        functools.partial(gate_up_body, rides),
        grid=(count,),
        in_specs=[
            pl.BlockSpec((n, rows, wide), lambda e: (0, 0, 0)),
            pl.BlockSpec((n, 1, rows, columns), lambda e: (0, e, 0, 0)),
        ]
        + rides.specs
        + [hbm] * len(others),
        out_specs=[
            pl.BlockSpec((1, width, columns), lambda e: (jnp.minimum(e, cut - 1), 0, 0)),
            pl.BlockSpec((1, width, columns), lambda e: (jnp.maximum(e - cut, 0), 0, 0)),
        ]
        + rides.specs,
        out_shape=[
            jax.ShapeDtypeStruct((cut, width, columns), BF16),
            jax.ShapeDtypeStruct((count - cut, width, columns), BF16),
        ]
        + rides.shapes,
        scratch_shapes=rides.scratch + [pltpu.VMEM((width, n * rows), BF16)],
        compiler_params=pltpu.CompilerParams(
            vmem_limit_bytes=44 * 2**20, has_side_effects=True, collective_id=identity
        ),
        cost_estimate=lasting(0.24),
    )(exts, grads, *rides.blocks, *others)
    return out[:2], out[2:]


def add(a, b):
    return (a.astype(F32) + b.astype(F32)).astype(BF16)


def one_of(block, index, dim):
    return lax.dynamic_slice_in_dim(block, index, 1, dim)


def opened(block):
    highs, rows, columns = block.shape
    n = lax.axis_size("expert")
    return block.reshape([2] * (len(bits_of("fsdp")) - 1) + [n, 2, rows // n // 2, columns])


ORDERS = ["yzx", "zyx"]


def owned_body(rides, cuts, *refs):
    bits = bits_of("fsdp")[:-1]
    n = lax.axis_size("expert")
    me, section, fsdp = lax.axis_index("expert"), lax.axis_index("section"), lax.axis_index("fsdp")
    axes = [("y", bit) for bit in bits] + [("z", None), ("x", None)]
    own = [(fsdp // bit) % 2 for bit in bits] + [me, section]
    orders = ORDERS
    block_ref, riding, refs = refs[0], refs[1 : 1 + rides.count], refs[1 + rides.count :]
    out_ref, arrived, refs = refs[0], refs[1 : 1 + rides.count], list(refs[1 + rides.count :])
    if rides.count:
        ride_sems = refs.pop(0)
    sems, refs = refs[0], refs[1:]
    meet()
    if rides.count:
        rides.start(riding, arrived, ride_sems)
    used = [0]

    def steps(part):
        current, landing = refs[part][0], refs[part][1:]
        done, made = set(), []
        slot = 0
        for letter in orders[part]:
            for dim, (name, bit) in enumerate(axes):
                if name != letter:
                    continue
                size = n if name == "z" else 2

                def region(index, dim=dim, finished=frozenset(done)):
                    return tuple(
                        index if d == dim else (own[d] if d in finished else slice(None))
                        for d in range(len(axes))
                    )

                copies = []
                for step in range(1, size):
                    if name == "z":
                        there = lax.rem(me + step, n)
                        device = {"expert": there}
                    elif name == "y":
                        there, device = 1 - own[dim], {"fsdp": fsdp ^ bit}
                    else:
                        there, device = 1 - section, {"section": 1 - section}
                    copies.append(
                        pltpu.make_async_remote_copy(
                            src_ref=current.at[region(there)], dst_ref=landing[slot],
                            send_sem=sems.at[0, used[0]], recv_sem=sems.at[1, used[0]],
                            device_id=device, device_id_type=MESH,
                        )
                    )
                    used[0] += 1
                    slot += 1

                def start(copies=copies):
                    for copy in copies:
                        copy.start()

                def finish(copies=copies, region=region, dim=dim, spots=range(slot - len(copies), slot)):
                    spot = region(own[dim])
                    total = current[spot].astype(F32)
                    for copy, k in zip(copies, spots):
                        copy.wait_recv()
                        total = total + landing[k][...].astype(F32)
                    for copy in copies:
                        copy.wait_send()
                    current[spot] = total.astype(BF16)

                made.append((start, finish))
                done.add(dim)
        return made

    plans = []
    for part, (low, high) in enumerate(cuts):
        refs[part][0][...] = block_ref[..., low:high]
        plans.append(steps(part))
        plans[-1][0][0]()
    for stage in range(len(plans[0])):
        for plan in plans:
            plan[stage][1]()
            if stage + 1 < len(plan):
                plan[stage + 1][0]()
    for part, (low, high) in enumerate(cuts):
        out_ref[:, low:high] = refs[part][0][tuple(own)]
    if rides.count:
        rides.finish(riding, arrived, ride_sems)


def owned_rows(block, rides, identity):
    rides = Rides(rides)
    bits = len(bits_of("fsdp")) - 1
    n = lax.axis_size("expert")
    rows, columns = block.shape[-2:]
    much = columns // LANES * 3 // 5 * LANES
    cuts = [(0, much), (much, columns)]
    scratch = [pltpu.SemaphoreType.DMA((2, len(cuts) * (bits + n)))]
    for (low, high), order in zip(cuts, ORDERS):
        shape = list(block.shape[:-1]) + [high - low]
        buffers = [pltpu.VMEM(tuple(shape), BF16)]
        for letter in order:
            for dim, name in enumerate(["y"] * bits + ["z", "x"]):
                if name == letter:
                    size = shape[dim]
                    shape[dim] = 0
                    landing = tuple(v for v in shape if v)
                    buffers += [pltpu.VMEM(landing, BF16)] * (size - 1)
        scratch.append(buffers)
    out = pl.pallas_call(
        functools.partial(owned_body, rides, cuts),
        in_specs=[pl.BlockSpec(memory_space=pltpu.VMEM)] + rides.specs,
        out_specs=[pl.BlockSpec(memory_space=pltpu.VMEM)] + rides.specs,
        out_shape=[jax.ShapeDtypeStruct((rows, columns), BF16)] + rides.shapes,
        scratch_shapes=rides.scratch + scratch,
        compiler_params=pltpu.CompilerParams(
            vmem_limit_bytes=48 * 2**20, has_side_effects=True, collective_id=identity
        ),
        cost_estimate=lasting(0.24),
    )(block, *rides.blocks)
    return out[0], out[1:]


def scatter_expert(block):
    return lax.psum_scatter(block, "fsdp", scatter_dimension=1, tiled=True)


def toward(block, target):
    return lax.ppermute(block, "section", [(1 - target, target)])


def shards(
    x_in, cotangent, seg_ids, routes, query_key_value_weight, w_out, w_router,
    norm1_gain, norm2_gain, w_gate_up, w_down,
):
    section = lax.axis_index("section")
    first = section == 0
    n = lax.axis_size("expert")
    n_total = w_router.shape[-1]
    rows, width = x_in.shape[1:]
    qkv_columns = query_key_value_weight.shape[-1]

    def by_section(block):
        other = swap(block, "section", 1)
        return jnp.where(first, block, other), jnp.where(first, other, block)

    tokens = pick(x_in, section)
    cot = pick(cotangent, section)
    segment = pick(seg_ids, section)
    packed = jnp.concatenate(
        [
            query_key_value_weight[0], w_router[0], norm1_gain[0][:, None], norm2_gain[0][:, None],
            jnp.zeros((w_router.shape[1], LANES - n_total - 2), BF16),
        ], 1,
    )
    packed = by_section(packed)
    outs = by_section(w_out[0])
    peer_route = swap(pick(routes[0], 1 - section), "section", 1)
    own_route = pick(routes[0], section)
    route = (jnp.where(first, own_route, peer_route), jnp.where(first, peer_route, own_route))
    layout = query_layout(segment, rows)
    down = lax.all_gather(w_down[0], ("section", "fsdp"), axis=0)
    gate_up = lax.all_gather(w_gate_up[0], ("section", "fsdp"), axis=0)

    qkv_pieces = Pieces(dense_pieces(packed[0], True))
    normed0, q0, kv0, small0, attended0, lse0, qkv0 = attention_forward(
        tokens, layout, qkv_pieces, n_total, 4
    )
    out_pieces = Pieces(dense_pieces(outs[0], True, lse0))
    hidden0, ext0, wout0 = route_tokens(tokens, attended0, small0, route[0], out_pieces, n_total)
    if len(bits_of("fsdp")) == 2 and packed[1].shape[0] % 32 == 0:
        qkv1, out1, grads1 = gather_next(packed[1], outs[1], cot, ext0)
        qkv_pieces, out_pieces = Pieces([(0, 0, qkv1)]), Pieces([(0, 0, out1)])
    else:
        qkv_pieces = Pieces(dense_pieces(tie(packed[1], q0), True))
        out_pieces = Pieces(dense_pieces(tie(outs[1], q0), True))
        grads1 = jnp.stack(ring_of(tie(cot, lse0)))
    summed, ring_x0, both0 = run_experts(
        "forward", 0, ext0, (), gate_up, down, (grads1, *qkv_pieces.blocks, *out_pieces.blocks)
    )
    out0 = (hidden0 + summed).astype(BF16)

    normed1, q1, kv1, small1, attended1, lse1, qkv1 = attention_forward(
        out0, layout, qkv_pieces, n_total, 12
    )
    hidden1, ext1, wout1 = route_tokens(out0, attended1, small1, route[1], out_pieces, n_total)
    summed, ring_x1, grad_both, act, parts = run_experts("both", 1, ext1, (grads1,), gate_up, down)

    grad_down = down_products(grads1, act)
    high_parts = [(parts[step], "expert", n - step) for step in range(1, n) if step != n // 2]
    (low, high), come = gate_up_products(
        ring_x1, grad_both, high_parts + [(out0, "section", 0)], 7, (grad_down,)
    )
    come, sent_out0 = come[:-1], come[-1]
    products1 = [grad_down, low, high]
    experts1 = [scatter_expert(p) for p in products1]
    grad_hidden, grad_attn, grad_attended, grad_logits1, gain_two1 = route_back(
        summed, tie(hidden1, *products1), ext1, cot, small1, wout1, n_total
    )
    grad_q, grad_kv, _ = attention_backward(q1, kv1, grad_attended, lse1, layout)
    grad_mixed1, grad1, gain_one1 = project_back(
        grad_q, grad_kv, layout[1], out0, grad_hidden, small1, qkv1, n_total
    )
    sum1 = opened(
        dense_product(
            normed1, grad_mixed1, n_total, (ext1, grad_logits1, gain_one1, gain_two1), (attended1, grad_attn)
        )
    )

    x_dim = sum1.ndim - 3
    crossing = one_of(sum1, 1 - section, x_dim)
    summed, grads0, grad_both, act = run_experts(
        "backward", 0, grad1, (ring_x0, both0), gate_up, down, (crossing,)
    )
    sum1 = add(one_of(sum1, section, x_dim), swap(crossing, "section", 1))
    grad_down = down_products(grads0, act, (sum1, *experts1))
    y_rides, fsdp = [], lax.axis_index("fsdp")
    bits = bits_of("fsdp")[:-1]
    if len(bits) == 1:
        mine = (fsdp // bits[0]) % 2
        y_rides = [(one_of(sum1, 1 - mine, 0), "fsdp", bits[0])]
    (low, high), crossed = gate_up_products(
        ring_x0, grad_both,
        [(parts[n // 2], "expert", n - n // 2), (experts1[2], "section", 1)] + y_rides,
        8, (grad_down,),
    )
    middle, sent_high1 = crossed[:2]
    if y_rides:
        sum1 = add(one_of(sum1, mine, 0), crossed[2])
    else:
        for dim, bit in enumerate(bits):
            mine = (fsdp // bit) % 2
            sum1 = add(one_of(sum1, mine, dim), swap(one_of(sum1, 1 - mine, dim), "fsdp", bit))
    experts0 = [scatter_expert(grad_down), scatter_expert(low)]
    out1 = hidden1 + parts[0].astype(F32) + middle.astype(F32)
    for part in come:
        out1 = out1 + part.astype(F32)
    out1 = out1.astype(BF16)
    grad_hidden, grad_attn, grad_attended, grad_logits0, gain_two0 = route_back(
        summed, tie(hidden0, grad_down, low), ext0, grad1, small0, wout0, n_total
    )
    experts0.append(scatter_expert(tie(high, experts0[0], grad_attended)))
    me, z_dim = lax.axis_index("expert"), sum1.ndim - 4
    z_rides = [
        (one_of(sum1, lax.rem(me + step, n), z_dim), "expert", step) for step in range(1, n)
    ]
    grad_q, grad_kv, crossed = attention_backward(
        q0, kv0, grad_attended, lse0, layout, z_rides + [(experts1[0], "section", 1), (experts0[0], "section", 0)], 9
    )
    half1 = one_of(sum1, me, z_dim).astype(F32)
    for part in crossed[: n - 1]:
        half1 = half1 + part.astype(F32)
    half1 = half1.astype(BF16).reshape(half1.shape[-2:])
    sent_down1, sent_down0 = crossed[n - 1 :]
    grad_mixed0, grad0, gain_one0 = project_back(
        grad_q, grad_kv, layout[1], tokens, grad_hidden, small0, qkv0, n_total
    )
    sum0 = opened(
        dense_product(
            normed0, grad_mixed0, n_total, (ext0, grad_logits0, gain_one0, gain_two0),
            (attended0, grad_attn),
        )
    )
    half0, crossed = owned_rows(
        sum0,
        (
            (experts0[1], "section", 0), (grad0, "section", 0), (experts1[1], "section", 1),
            (half1, "section", 1), (out1, "section", 1), (grad1, "section", 1),
        ),
        10,
    )
    sent_low0, sent_grad0, sent_low1, sent_half1, sent_out1, sent_grad1 = crossed
    sent0 = [sent_down0, sent_low0, toward(experts0[2], 0)]
    sent1 = [sent_down1, sent_low1, sent_high1]

    def stacked(a0, a1, came0, came1):
        mine, other = jnp.where(first, a0, a1), jnp.where(first, came0, came1)
        return jnp.stack([jnp.where(first, mine, other), jnp.where(first, other, mine)])[None]

    section_out = stacked(out0, out1, sent_out0, sent_out1)
    in_grad = stacked(grad0, grad1, sent_grad0, sent_grad1)
    grad_down, gate_up_low, gate_up_high = [
        jnp.where(first, b0, b1).astype(F32) + jnp.where(first, r0, r1).astype(F32)
        for b0, b1, r0, r1 in zip(experts0, experts1, sent0, sent1)
    ]
    other = jnp.where(first, toward(half0, 0), sent_half1).astype(F32)
    own = jnp.where(first, half0, half1).astype(F32)
    grad_dense = jnp.concatenate([jnp.where(first, own, other), jnp.where(first, other, own)], 0)
    grad_packed, grad_w_out = grad_dense[:, : qkv_columns + LANES], grad_dense[:, qkv_columns + LANES :]
    grad_gate_up = jnp.concatenate([gate_up_low, gate_up_high], 0)
    return (
        section_out,
        in_grad,
        grad_packed[:, :qkv_columns][None],
        grad_w_out[None],
        grad_packed[:, qkv_columns : qkv_columns + n_total][None],
        grad_packed[:, qkv_columns + n_total][None],
        grad_packed[:, qkv_columns + n_total + 1][None],
        grad_gate_up[None],
        grad_down[None],
    )


def solution(mesh):
    both = ("fsdp", "expert")
    weights = (
        P("section", both, None),
        P("section", both, None),
        P("section", both, None),
        P("section", both),
        P("section", both),
        P("section", "expert", "fsdp", None),
        P("section", "expert", "fsdp", None),
    )
    return jax.shard_map(
        shards,
        mesh=mesh,
        in_specs=(
            P(None, both, None),
            P(None, both, None),
            P(None, "fsdp"),
            P("section", None, both, None),
        )
        + weights,
        out_specs=(P("section", None, both, None), P("section", None, both, None)) + weights,
        check_vma=False,
    )
```
